256 devices in a mesh: seq: 32 (over z, y), head: 4 (over x), rep: 2 (over core).
Axes of the slice: x: 4, y: 4, z: 8, core: 2. Of those that a mesh axis runs over, the one named last changes fastest.
Arguments:
- queries: bfloat16 [16384, 2048], P(('rep', 'seq'), 'head'), parts along dimension 0, may hold values from -5 to 5
- keys: bfloat16 [16384, 2048], P(('rep', 'seq'), 'head'), parts along dimension 0, may hold values from -5 to 5
- values: bfloat16 [16384, 2048], P(('rep', 'seq'), 'head'), parts along dimension 0, may hold values from -4 to 4
- cotangent: bfloat16 [16384, 2048], P(('rep', 'seq'), 'head'), parts along dimension 0, may hold values from -4 to 4
Outputs:
- attended: bfloat16 [16384, 2048], P(('rep', 'seq'), 'head'), parts along dimension 0
- grad_queries: bfloat16 [16384, 2048], P(('rep', 'seq'), 'head'), parts along dimension 0
- grad_keys: bfloat16 [16384, 2048], P(('rep', 'seq'), 'head'), parts along dimension 0
- grad_values: bfloat16 [16384, 2048], P(('rep', 'seq'), 'head'), parts along dimension 0
The draws below stay inside these ranges and needn't reach their ends.
There are 2 independent parts, one for each index of `rep`. The reference program is written for one: setup_inputs(seed, part) draws one part's arguments, and reference() takes and returns one part's arrays. A program takes and returns all parts, laid end to end along the dimension named above; each array names one. Nothing has to cross between parts.
All inputs are finite; a program needn't handle non-finite values.
Results may differ from the reference program's by a relative error of at most 0.012.
Values may be sent and summed in bfloat16 or wider, within the bound.
No kernel may reach another device: no remote copies, remote signals or barrier semaphores. Data moves between devices by JAX's collectives and lax.ppermute only.
A program may use at most 128 MiB of HBM per device.

```python
import math
import jax
import jax.numpy as jnp
from jax import lax

HEADS = 16
HEAD_DIM = 128
BLOCK = 128
WIDTH = 2048
TOKENS = 8192


def draw_queries(key, part):
    key = jax.random.fold_in(key, 1)
    normal_part = jnp.clip(jax.random.normal(key, (TOKENS, WIDTH), jnp.float32), -4.0, 4.0)
    return normal_part.astype(jnp.bfloat16)


def draw_keys(key, part):
    key = jax.random.fold_in(key, 2)
    normal_part = jnp.clip(jax.random.normal(key, (TOKENS, WIDTH), jnp.float32), -4.0, 4.0)
    return normal_part.astype(jnp.bfloat16)


def levels(own_key, shape, shards, low, largest):
    gain = 1.0
    for dim, blocks in shards:
        steps = jax.random.uniform(jax.random.fold_in(jax.random.fold_in(own_key, 6), dim), (blocks,), jnp.float32, low / len(shards), largest / len(shards))
        gain = gain * jnp.repeat(jnp.exp(steps), shape[dim] // blocks).reshape((-1,) + (1,) * (len(shape) - 1 - dim))
    return gain


def normal_values(stream_key, extent, deviation, limit, split=(), held_as=jnp.bfloat16):
    level = levels(stream_key, extent, split, -0.22, 0.18) if split else 1.0
    drawn = jax.random.normal(stream_key, extent, jnp.float32) * deviation * level
    return jnp.minimum(jnp.maximum(drawn, -limit), limit).astype(held_as)


def setup_inputs(seed: int = 0, part: int = 0) -> dict:
    splits = jax.random.split(jax.random.key(seed), 5)
    part_keys = jax.random.split(jax.random.fold_in(splits[4], part), 5)
    queries = draw_queries(jax.random.fold_in(jax.random.fold_in(splits[4], part), 71), part)
    keys = draw_keys(jax.random.fold_in(jax.random.fold_in(splits[4], part), 71), part)
    values = normal_values(part_keys[2], (TOKENS, WIDTH), 1.0, 4.0, ((0, 32), (1, 4)))
    cotangent = normal_values(part_keys[3], (TOKENS, WIDTH), 1.0, 4.0, ((0, 32), (1, 4)))
    return dict(queries=queries, keys=keys, values=values, cotangent=cotangent)


ROOT_HALF = 0.7071067811865476

def pooled(stacked):
    paired = stacked.astype(jnp.float32).reshape(stacked.shape[0] // 2, 2, stacked.shape[1])
    return ((paired[:, 0] + paired[:, 1]) * ROOT_HALF).astype(jnp.bfloat16)

def spread(gradients):
    return jnp.repeat(gradients * ROOT_HALF, 2, axis=0)

def one_head(queries, keys, values, cotangent):
    block_count = TOKENS // BLOCK
    depth = block_count.bit_length() - 1
    score_scale = 1.0 / math.sqrt(HEAD_DIM)
    coarse_keys = [keys]
    coarse_values = [values]
    for height in range(1, depth):
        coarse_keys.append(pooled(coarse_keys[-1]))
        coarse_values.append(pooled(coarse_values[-1]))
    margin = jnp.zeros((BLOCK, HEAD_DIM), jnp.bfloat16)
    padded_keys = jnp.concatenate([margin, keys, margin])
    padded_values = jnp.concatenate([margin, values, margin])
    key_count = (depth + 2) * BLOCK
    column_ids = jnp.arange(key_count, dtype=jnp.int32)
    initial = (jnp.zeros((TOKENS + 2 * BLOCK, HEAD_DIM), jnp.float32), jnp.zeros((TOKENS + 2 * BLOCK, HEAD_DIM), jnp.float32), tuple((jnp.zeros((TOKENS >> height, HEAD_DIM), jnp.float32) for height in range(1, depth))), tuple((jnp.zeros((TOKENS >> height, HEAD_DIM), jnp.float32) for height in range(1, depth))))

    def visit(carried_state, block_no):
        pad_key_grads, pad_value_grads, level_key_grads, level_value_grads = carried_state
        first_row = block_no * BLOCK
        query_rows = lax.dynamic_slice_in_dim(queries, first_row, BLOCK, 0)
        cot_rows = lax.dynamic_slice_in_dim(cotangent, first_row, BLOCK, 0)
        key_parts = [lax.dynamic_slice_in_dim(padded_keys, first_row, 3 * BLOCK, 0)]
        value_parts = [lax.dynamic_slice_in_dim(padded_values, first_row, 3 * BLOCK, 0)]
        sibling_rows = []
        for height in range(1, depth):
            sibling = jnp.bitwise_xor(block_no // 2 ** height, 1).astype(jnp.int32) * BLOCK
            sibling_rows.append(sibling)
            key_parts.append(lax.dynamic_slice_in_dim(coarse_keys[height], sibling, BLOCK, 0))
            value_parts.append(lax.dynamic_slice_in_dim(coarse_values[height], sibling, BLOCK, 0))
        all_keys = jnp.concatenate(key_parts)
        all_values = jnp.concatenate(value_parts)
        scores = jnp.dot(query_rows, all_keys.T, preferred_element_type=jnp.float32) * score_scale
        allowed = ((column_ids >= BLOCK) | (block_no > 0)) & ((column_ids < 2 * BLOCK) | (column_ids >= 3 * BLOCK) | (block_no < block_count - 1))
        scores = jnp.where(allowed[None, :], scores, -jnp.inf)
        highest = lax.optimization_barrier(jnp.max(scores, axis=1, keepdims=True))
        raised = jnp.exp(scores - highest)
        denominator = lax.optimization_barrier(jnp.sum(raised, axis=1, keepdims=True))
        probability = raised / denominator
        weights = probability.astype(jnp.bfloat16)
        output = jnp.dot(weights, all_values, preferred_element_type=jnp.float32)
        row_dot = lax.optimization_barrier(jnp.sum(cot_rows.astype(jnp.float32) * output, axis=1, keepdims=True))
        prob_grad = jnp.dot(cot_rows, all_values.T, preferred_element_type=jnp.float32)
        score_grad = (probability * (prob_grad - row_dot) * score_scale).astype(jnp.bfloat16)
        query_grad = jnp.dot(score_grad, all_keys, preferred_element_type=jnp.float32)
        key_grads = jnp.dot(score_grad.T, query_rows, preferred_element_type=jnp.float32)
        value_grads = jnp.dot(weights.T, cot_rows, preferred_element_type=jnp.float32)
        pad_key_grads = lax.dynamic_update_slice_in_dim(pad_key_grads, lax.dynamic_slice_in_dim(pad_key_grads, first_row, 3 * BLOCK, 0) + key_grads[:3 * BLOCK], first_row, 0)
        pad_value_grads = lax.dynamic_update_slice_in_dim(pad_value_grads, lax.dynamic_slice_in_dim(pad_value_grads, first_row, 3 * BLOCK, 0) + value_grads[:3 * BLOCK], first_row, 0)
        new_key_levels = []
        new_value_levels = []
        for position in range(depth - 1):
            height = position + 1
            sibling = sibling_rows[position]
            start_col = (2 + height) * BLOCK
            held_keys = level_key_grads[position]
            held_values = level_value_grads[position]
            new_key_levels.append(lax.dynamic_update_slice_in_dim(held_keys, lax.dynamic_slice_in_dim(held_keys, sibling, BLOCK, 0) + key_grads[start_col:start_col + BLOCK], sibling, 0))
            new_value_levels.append(lax.dynamic_update_slice_in_dim(held_values, lax.dynamic_slice_in_dim(held_values, sibling, BLOCK, 0) + value_grads[start_col:start_col + BLOCK], sibling, 0))
        new_state = (pad_key_grads, pad_value_grads, tuple(new_key_levels), tuple(new_value_levels))
        return (new_state, (output.astype(jnp.bfloat16), query_grad.astype(jnp.bfloat16)))
    final_state, stacked_out = lax.scan(visit, initial, jnp.arange(block_count, dtype=jnp.int32))
    pad_key_grads, pad_value_grads, level_key_grads, level_value_grads = final_state
    attended = stacked_out[0].reshape(TOKENS, HEAD_DIM)
    grad_queries = stacked_out[1].reshape(TOKENS, HEAD_DIM)
    upward_keys = level_key_grads[depth - 2]
    upward_values = level_value_grads[depth - 2]
    for height in reversed(range(1, depth - 1)):
        upward_keys = level_key_grads[height - 1] + spread(upward_keys)
        upward_values = level_value_grads[height - 1] + spread(upward_values)
    grad_keys = (pad_key_grads[BLOCK:-BLOCK] + spread(upward_keys)).astype(jnp.bfloat16)
    grad_values = (pad_value_grads[BLOCK:-BLOCK] + spread(upward_values)).astype(jnp.bfloat16)
    return (attended, grad_queries, grad_keys, grad_values)

def by_heads(stacked):
    return stacked.reshape(TOKENS, HEADS, HEAD_DIM).transpose(1, 0, 2)

def from_heads(stacked):
    return stacked.transpose(1, 0, 2).reshape(TOKENS, HEADS * HEAD_DIM)

def per_head(members):
    return one_head(members[0], members[1], members[2], members[3])

def reference(queries, keys, values, cotangent):
    results = lax.map(per_head, (by_heads(queries), by_heads(keys), by_heads(values), by_heads(cotangent)))
    return (from_heads(results[0]), from_heads(results[1]), from_heads(results[2]), from_heads(results[3]))
```

```python
import functools
import math

import jax
import jax.numpy as jnp
from jax import lax
from jax.experimental import pallas as pl
from jax.experimental.pallas import tpu as pltpu
from jax.sharding import Mesh
from jax.sharding import PartitionSpec as P

D = 128
B = 128
NY = 4
NZ = 8
PIECE = 2 * B
PLANE = NY * PIECE
ROOT_HALF = 0.7071067811865476
SCALE = 1.0 / math.sqrt(D)
SCALE_LOG2E = SCALE * math.log2(math.e)
BF = jnp.bfloat16
F32 = jnp.float32

EXT = PLANE + 2 * B
AT1 = EXT
AT2 = AT1 + PLANE // 2
AT3 = AT2 + PLANE // 4
ROWS = AT3 + 3 * B

Z_SIDE = [(0, 6), (1, 7), (2, 4), (3, 5)]
TOP = Z_SIDE + [(b, a) for a, b in Z_SIDE]


def dot(a, b, ca=1, cb=0):
    return lax.dot_general(a, b, (((ca,), (cb,)), ((), ())), preferred_element_type=F32)


def pair_sum(rows):
    r = lax.broadcasted_iota(jnp.int32, (rows, 2 * rows), 0)
    c = lax.broadcasted_iota(jnp.int32, (rows, 2 * rows), 1)
    return (lax.shift_right_logical(c, 1) == r).astype(F32).astype(BF)


def repeat_matrix(rows, log):
    r = lax.broadcasted_iota(jnp.int32, (rows << log, rows), 0)
    c = lax.broadcasted_iota(jnp.int32, (rows << log, rows), 1)
    return (lax.shift_right_logical(r, log) == c).astype(F32).astype(BF)


def pool(matrix, x):
    return (dot(matrix, x) * ROOT_HALF).astype(BF)


def expand(matrix, x):
    high = x.astype(BF)
    low = (x - high.astype(F32)).astype(BF)
    return dot(matrix, high) + dot(matrix, low)


def piece_at(index):
    return pl.ds(pl.multiple_of(index * PIECE, PIECE), PIECE)


def head_at(index):
    return pl.ds(pl.multiple_of(index * D, D), D)


def pack_kernel(at_ref, left_ref, right_ref, *outs):
    y = at_ref[0]
    for d in range(NY):
        head = lax.rem(y + d, NY)
        outs[d][:, :D] = left_ref[:, head_at(head)]
        outs[d][:, D:] = right_ref[:, head_at(head)]


def pool_kernel(at_ref, k0, k1, k2, k3, all_ref, one_ref, two_ref, three_ref, low_ref, high_ref):
    y = at_ref[0]
    for d, ref in enumerate((k0, k1, k2, k3)):
        all_ref[piece_at(lax.rem(y - d + NY, NY)), :] = ref[...]
    matrix = pair_sum(B)
    for n in range(4):
        one_ref[n * B : (n + 1) * B] = pool(matrix, all_ref[n * PIECE : (n + 1) * PIECE])
    for n in range(2):
        two_ref[n * B : (n + 1) * B] = pool(matrix, one_ref[n * PIECE : (n + 1) * PIECE])
    three_ref[...] = pool(matrix, two_ref[...])
    low_ref[...] = all_ref[:B]
    high_ref[...] = all_ref[PLANE - B :]


def climb_kernel(which, at_ref, own_ref, other_ref, out_ref):
    bit = lax.rem(lax.shift_right_logical(at_ref[1], which), 2)
    half = B // 2
    matrix = pair_sum(half)
    out_ref[pl.ds(pl.multiple_of(bit * half, half), half), :] = pool(matrix, own_ref[...])
    out_ref[pl.ds(pl.multiple_of((1 - bit) * half, half), half), :] = pool(matrix, other_ref[...])


def attend_kernel(
    at_ref, kv, one, two, edge_low, edge_high, far3, far4, far5, q0, q1, q2, q3,
    og0, og1, og2, og3, g_low, g_high, g5, g4, g3, g_own, g_one, g_two,
    keys, vals, keys_t, vals_t, qc, og, grads,
):
    y = at_ref[0]
    z = at_ref[1]
    for d, ref in enumerate((q0, q1, q2, q3)):
        qc[piece_at(lax.rem(y - d + NY, NY)), :] = ref[...]
    at = 0
    for ref in (edge_low, kv, edge_high, one, two, far3, far4, far5):
        rows = ref.shape[0]
        keys[at : at + rows, :] = ref[:, :D]
        vals[at : at + rows, :] = ref[:, D:]
        at += rows
    for n in range(ROWS // B):
        cut = slice(n * B, (n + 1) * B)
        keys_t[:, cut] = keys[cut, :].T
        vals_t[:, cut] = vals[cut, :].T
    grads[...] = jnp.zeros_like(grads)

    second = lax.broadcasted_iota(jnp.int32, (B, PIECE), 1) >= B

    def visit(i, _):
        near = pl.multiple_of(i * PIECE, PIECE)
        pieces = (
            (near, 4 * B),
            (pl.multiple_of(AT1 + (i ^ 1) * B, B), B),
            (pl.multiple_of(AT2 + (lax.shift_right_logical(i, 1) ^ 1) * B, B), B),
            (AT3, 3 * B),
        )
        q = qc[piece_at(i), :D]
        c = qc[piece_at(i), D:]
        scores = [dot(keys[pl.ds(a, n), :], q, 1, 1) for a, n in pieces]
        no_low = (z == 0) & (i == 0)
        no_high = (z == NZ - 1) & (i == NY - 1)
        first = jnp.where(second | no_low, -jnp.inf, scores[0][:B])
        last = jnp.where(second, jnp.where(no_high, -jnp.inf, scores[0][3 * B :]), -jnp.inf)
        scores[0] = jnp.concatenate([first, scores[0][B : 3 * B], last], axis=0)
        top = functools.reduce(jnp.maximum, [jnp.max(s, axis=0, keepdims=True) for s in scores])
        raised = [jnp.exp2((s - top) * SCALE_LOG2E) for s in scores]
        total = functools.reduce(jnp.add, [jnp.sum(e, axis=0, keepdims=True) for e in raised])
        inverse = 1.0 / total
        probs = [e * inverse for e in raised]
        weights = [p.astype(BF) for p in probs]
        pgrads = [dot(vals[pl.ds(a, n), :], c, 1, 1) for a, n in pieces]
        row_dot = functools.reduce(
            jnp.add,
            [jnp.sum(w.astype(F32) * g, axis=0, keepdims=True) for w, g in zip(weights, pgrads)],
        )
        sgrads = [(p * (g - row_dot) * SCALE).astype(BF) for p, g in zip(probs, pgrads)]
        out_t = functools.reduce(
            jnp.add, [dot(vals_t[:, pl.ds(a, n)], w) for (a, n), w in zip(pieces, weights)]
        )
        qg_t = functools.reduce(
            jnp.add, [dot(keys_t[:, pl.ds(a, n)], s) for (a, n), s in zip(pieces, sgrads)]
        )
        og[piece_at(i), :D] = out_t.T.astype(BF)
        og[piece_at(i), D:] = qg_t.T.astype(BF)
        for (a, n), w, s in zip(pieces, weights, sgrads):
            grads[pl.ds(a, n), :D] += dot(s, q)
            grads[pl.ds(a, n), D:] += dot(w, c)
        return 0

    lax.fori_loop(0, NY, visit, 0)
    for d, ref in enumerate((og0, og1, og2, og3)):
        ref[...] = og[piece_at(lax.rem(y + d, NY)), :]
    g_low[...] = grads[:B].astype(BF)
    g_high[...] = grads[EXT - B : EXT].astype(BF)
    g3[...] = grads[AT3 : AT3 + B]
    g4[...] = grads[AT3 + B : AT3 + 2 * B]
    g5[...] = grads[AT3 + 2 * B :].astype(BF)
    g_own[...] = grads[B : EXT - B]
    g_one[...] = grads[AT1:AT2]
    g_two[...] = grads[AT2:AT3]


def local_kernel(own_ref, one_ref, two_ref, out_ref):
    matrix = repeat_matrix(B, 1)
    for n in range(2):
        two = expand(matrix, two_ref[n * B : (n + 1) * B] * ROOT_HALF)
        for m in range(2):
            k = 2 * n + m
            one = one_ref[k * B : (k + 1) * B] + two[m * B : (m + 1) * B]
            cut = slice(k * PIECE, (k + 1) * PIECE)
            out_ref[cut] = own_ref[cut] + expand(matrix, one * ROOT_HALF)


def halves(bit):
    half = B // 2
    own = pl.ds(pl.multiple_of(bit * half, half), half)
    other = pl.ds(pl.multiple_of((1 - bit) * half, half), half)
    return own, other


def descend_top_kernel(at_ref, back_ref, mine_ref, send_ref, keep_ref):
    own, other = halves(lax.rem(lax.shift_right_logical(at_ref[1], 1), 2))
    matrix = repeat_matrix(B // 2, 1)
    send_ref[...] = (mine_ref[...] + dot(matrix, back_ref[other, :]) * ROOT_HALF).astype(BF)
    keep_ref[...] = dot(matrix, back_ref[own, :]) * ROOT_HALF


def descend_kernel(at_ref, back_ref, kept_ref, mine_ref, send_ref, keep_ref):
    own, other = halves(lax.rem(at_ref[1], 2))
    matrix = repeat_matrix(B // 2, 1)

    def half_of(cut):
        return expand(matrix, (kept_ref[cut, :] + back_ref[cut, :].astype(F32)) * ROOT_HALF)

    send_ref[...] = (mine_ref[...] + half_of(other)).astype(BF)
    keep_ref[...] = half_of(own)


def final_kernel(at_ref, own_ref, low_ref, high_ref, back_ref, kept_ref, f0, f1, f2, f3, total):
    y = at_ref[0]
    matrix = repeat_matrix(B // NY, 3)
    up = (kept_ref[...] + back_ref[...].astype(F32)) * (ROOT_HALF * 0.5)
    for n in range(NY):
        rows = B // NY
        cut = slice(n * PIECE, (n + 1) * PIECE)
        total[cut] = own_ref[cut] + expand(matrix, up[n * rows : (n + 1) * rows])
    total[:B] += low_ref[...].astype(F32)
    total[PLANE - B :] += high_ref[...].astype(F32)
    for d, ref in enumerate((f0, f1, f2, f3)):
        ref[...] = total[piece_at(lax.rem(y + d, NY)), :].astype(BF)


def unpack_kernel(at_ref, r0, r1, r2, r3, left_ref, right_ref):
    y = at_ref[0]
    for d, ref in enumerate((r0, r1, r2, r3)):
        head = head_at(lax.rem(y - d + NY, NY))
        left_ref[:, head] = ref[:, :D]
        right_ref[:, head] = ref[:, D:]


def call(kernel, ins, outs, scratch=(), scalars=True, flops=10**6):
    vmem = pl.BlockSpec(memory_space=pltpu.VMEM)
    smem = pl.BlockSpec(memory_space=pltpu.SMEM)
    arrays = ins[1:] if scalars else ins
    size = sum(a.size * a.dtype.itemsize for a in arrays)
    size += sum(math.prod(s) * jnp.dtype(t).itemsize for s, t in outs)
    return pl.pallas_call(
        kernel,
        out_shape=[jax.ShapeDtypeStruct(s, t) for s, t in outs],
        in_specs=([smem] if scalars else []) + [vmem] * len(arrays),
        out_specs=[vmem] * len(outs),
        scratch_shapes=list(scratch),
        compiler_params=pltpu.CompilerParams(vmem_limit_bytes=40 * 2**20),
        cost_estimate=pl.CostEstimate(flops=flops, bytes_accessed=size, transcendentals=0),
    )(*ins)


def around_y(pieces):
    got = [pieces[0]]
    for d in range(1, NY):
        got.append(lax.ppermute(pieces[d], "y", [(i, (i + d) % NY) for i in range(NY)]))
    return got


def over_z(array, bit):
    return lax.ppermute(array, "z", [(i, i ^ (1 << bit)) for i in range(NZ)])


def up_z(array):
    return lax.ppermute(array, "z", [(i, i + 1) for i in range(NZ - 1)])


def down_z(array):
    return lax.ppermute(array, "z", [(i + 1, i) for i in range(NZ - 1)])


def per_device(queries, keys, values, cotangent):
    at = jnp.stack([lax.axis_index("y"), lax.axis_index("z")]).astype(jnp.int32)
    piece = ((PIECE, 2 * D), BF)
    level = ((B, 2 * D), BF)
    wide = ((B, 2 * D), F32)
    kv = around_y(call(pack_kernel, [at, keys, values], [piece] * NY))
    qc = around_y(call(pack_kernel, [at, queries, cotangent], [piece] * NY))
    kv_all, one, two, three, low, high = call(
        pool_kernel,
        [at, *kv],
        [((PLANE, 2 * D), BF), ((PLANE // 2, 2 * D), BF), ((PLANE // 4, 2 * D), BF), level, level, level],
    )
    far3 = over_z(three, 0)
    edge_low = up_z(high)
    edge_high = down_z(low)
    (four,) = call(functools.partial(climb_kernel, 0), [at, three, far3], [level])
    far4 = over_z(four, 1)
    (five,) = call(functools.partial(climb_kernel, 1), [at, four, far4], [level])
    far5 = lax.ppermute(five, "z", TOP)
    *og, g_low, g_high, g5, g4, g3, g_own, g_one, g_two = call(
        attend_kernel,
        [at, kv_all, one, two, edge_low, edge_high, far3, far4, far5, *qc],
        [piece] * NY
        + [level, level, level, wide, wide]
        + [((PLANE, 2 * D), F32), ((PLANE // 2, 2 * D), F32), ((PLANE // 4, 2 * D), F32)],
        scratch=[
            pltpu.VMEM((ROWS, D), BF),
            pltpu.VMEM((ROWS, D), BF),
            pltpu.VMEM((D, ROWS), BF),
            pltpu.VMEM((D, ROWS), BF),
            pltpu.VMEM((PLANE, 2 * D), BF),
            pltpu.VMEM((PLANE, 2 * D), BF),
            pltpu.VMEM((ROWS, 2 * D), F32),
        ],
        flops=2 * 10**9,
    )
    back5 = lax.ppermute(g5, "z", TOP)
    from_low = up_z(g_high)
    from_high = down_z(g_low)
    og = around_y(og)
    send4, keep4 = call(descend_top_kernel, [at, back5, g4], [level, wide])
    back4 = over_z(send4, 1)
    send3, keep3 = call(descend_kernel, [at, back4, keep4, g3], [level, wide])
    back3 = over_z(send3, 0)
    (own,) = call(
        local_kernel, [g_own, g_one, g_two], [((PLANE, 2 * D), F32)], scalars=False
    )
    final = call(
        final_kernel,
        [at, own, from_low, from_high, back3, keep3],
        [piece] * NY,
        scratch=[pltpu.VMEM((PLANE, 2 * D), F32)],
    )
    final = around_y(final)
    whole = ((PIECE, NY * D), BF)
    attended, grad_queries = call(unpack_kernel, [at, *og], [whole] * 2)
    grad_keys, grad_values = call(unpack_kernel, [at, *final], [whole] * 2)
    return attended, grad_queries, grad_keys, grad_values


def solution(mesh):
    seq, head, rep = mesh.devices.shape
    split = Mesh(mesh.devices.reshape(NZ, NY, head, rep), ("z", "y", "head", "rep"))
    spec = P(("rep", "z", "y"), "head")
    return jax.shard_map(
        per_device, mesh=split, in_specs=(spec,) * 4, out_specs=(spec,) * 4, check_vma=False
    )
```

```python
import functools
import math

import jax
import jax.numpy as jnp
from jax import lax
from jax.experimental import pallas as pl
from jax.experimental.pallas import tpu as pltpu
from jax.sharding import Mesh
from jax.sharding import PartitionSpec as P

D = 128
B = 128
HALF = B // 2
NY = 4
NZ = 8
PIECE = 2 * B
PLANE = NY * PIECE
SMALL = PIECE // 8
Y_ORDER = (1, 2, 3)
EARLY_OUT = False
POOL = 5 * 10**9
FINAL = 5*10**9
EARLY_STACK = True
ROOT_HALF = 0.7071067811865476
SCALE = 1.0 / math.sqrt(D)
SCALE_LOG2E = SCALE * math.log2(math.e)
BF = jnp.bfloat16
F32 = jnp.float32

AT1 = PLANE
AT2 = AT1 + PLANE // 2
AT3 = AT2 + PLANE // 4
COLS = AT3 + 2 * B
PAIR = 8 * B


def dot(a, b, ca=1, cb=0):
    return lax.dot_general(a, b, (((ca,), (cb,)), ((), ())), preferred_element_type=F32)


def pair_sum(rows):
    r = lax.broadcasted_iota(jnp.int32, (rows, 2 * rows), 0)
    c = lax.broadcasted_iota(jnp.int32, (rows, 2 * rows), 1)
    return (lax.shift_right_logical(c, 1) == r).astype(F32).astype(BF)


def repeat_matrix(rows, log):
    r = lax.broadcasted_iota(jnp.int32, (rows << log, rows), 0)
    c = lax.broadcasted_iota(jnp.int32, (rows << log, rows), 1)
    return (lax.shift_right_logical(r, log) == c).astype(F32).astype(BF)


def pool(matrix, x):
    return (dot(matrix, x) * ROOT_HALF).astype(BF)


def expand(matrix, x):
    high = x.astype(BF)
    low = (x - high.astype(F32)).astype(BF)
    return dot(matrix, high) + dot(matrix, low)


def part_at(index, size=PIECE):
    return pl.ds(pl.multiple_of(index * size, size), size)


def head_at(index):
    return pl.ds(pl.multiple_of(index * D, D), D)


def later(y, d):
    return lax.rem(y + d, NY)


def earlier(y, d):
    return lax.rem(y - d + NY, NY)


def pack_kernel(at_ref, left_hbm, right_hbm, *refs):
    outs, sems = refs[:NY], refs[-1]
    y = at_ref[0]
    copies = [
        pltpu.make_async_copy(
            src.at[:, head_at(later(y, d))], outs[d].at[:, n * D : (n + 1) * D], sems.at[d, n]
        )
        for d in range(NY)
        for n, src in enumerate((left_hbm, right_hbm))
    ]
    for copy in copies:
        copy.start()
    for copy in copies:
        copy.wait()


def stack_kernel(at_ref, left_hbm, right_hbm, out_ref, sems):
    copies = [
        pltpu.make_async_copy(
            src.at[:, h * D : (h + 1) * D],
            out_ref.at[h * PIECE : (h + 1) * PIECE, n * D : (n + 1) * D],
            sems.at[h, n],
        )
        for h in range(NY)
        for n, src in enumerate((left_hbm, right_hbm))
    ]
    for copy in copies:
        copy.start()
    for copy in copies:
        copy.wait()


def unstack_kernel(at_ref, in_ref, left_hbm, right_hbm, token_ref, sems):
    token_ref[...] = jnp.zeros_like(token_ref)
    copies = [
        pltpu.make_async_copy(
            in_ref.at[h * PIECE : (h + 1) * PIECE, n * D : (n + 1) * D],
            dst.at[:, h * D : (h + 1) * D],
            sems.at[h, n],
        )
        for h in range(NY)
        for n, dst in enumerate((left_hbm, right_hbm))
    ]
    for copy in copies:
        copy.start()
    for copy in copies:
        copy.wait()


def unpack_kernel(at_ref, *refs):
    pieces, left_hbm, right_hbm, sems = refs[:NY], refs[NY], refs[NY + 1], refs[-1]
    y = at_ref[0]
    copies = [
        pltpu.make_async_copy(
            pieces[d].at[:, n * D : (n + 1) * D], dst.at[:, head_at(earlier(y, d))], sems.at[d, n]
        )
        for d in range(NY)
        for n, dst in enumerate((left_hbm, right_hbm))
    ]
    for copy in copies:
        copy.start()
    for copy in copies:
        copy.wait()


def pool_kernel(at_ref, k0, k1, k2, k3, kv_ref, m1_ref, m2_ref, m3_ref, tail_ref):
    y = at_ref[0]
    odd = lax.rem(at_ref[1], 2)
    for d, ref in enumerate((k0, k1, k2, k3)):
        kv_ref[part_at(earlier(y, d)), :] = ref[...]
    matrix = pair_sum(B)
    one = [pool(matrix, kv_ref[n * PIECE : (n + 1) * PIECE]) for n in range(4)]
    two = [pool(matrix, jnp.concatenate(one[n : n + 2], axis=0)) for n in (0, 2)]
    three = pool(matrix, jnp.concatenate(two, axis=0))
    four = pool(matrix[:HALF, :B], three)
    facing = kv_ref[part_at((1 - odd) * (PLANE // B - 1), B), :]
    other = kv_ref[part_at(odd * (PLANE // B - 1), B), :]
    m1_ref[:B] = three
    m1_ref[B:] = facing
    m2_ref[...] = four
    m3_ref[:HALF] = four
    m3_ref[HALF:] = other
    tail_ref[:HALF] = four
    tail_ref[HALF:] = other


def quad_kernel(at_ref, tail_ref, three_1, four_2, four_3, top_ref):
    z = at_ref[1]
    matrix = pair_sum(HALF)
    small = matrix[: B // 4, :HALF]
    fours = (tail_ref[:HALF], pool(matrix, three_1[:B]), four_2[...], four_3[:HALF])
    for d, four in enumerate(fours):
        top_ref[part_at((z ^ d) & 3, SMALL), :] = pool(small, four)
    top_ref[B:] = tail_ref[HALF:]


def by_three(z):
    return lax.rem(lax.shift_right_logical(z + 1, 1), 2) == 1


def pieces_of(i):
    start = max(0, i * PIECE - B)
    stop = min(PLANE, i * PIECE + 3 * B)
    return (
        (start, stop - start, start - (i * PIECE - B)),
        (AT1 + (i ^ 1) * B, B, 4 * B),
        (AT2 + ((i >> 1) ^ 1) * B, B, 5 * B),
        (AT3, 2 * B, 6 * B),
    )


def summed(values):
    return functools.reduce(jnp.add, values)


def early_kernel(
    at_ref, kv, from_1, from_2, from_3, qc, keys_t, vals_t, raised, pgrads, stats, keys, vals
):
    matrix = pair_sum(B)
    one = [pool(matrix, kv[n * PIECE : (n + 1) * PIECE]) for n in range(4)]
    two = [pool(matrix, jnp.concatenate(one[n : n + 2], axis=0)) for n in (0, 2)]
    at = 0
    for part in (kv[...], *one, *two, from_1[:B], from_2[...], from_3[:HALF]):
        rows = part.shape[0]
        keys[at : at + rows, :] = part[:, :D]
        vals[at : at + rows, :] = part[:, D:]
        at += rows
    second = lax.broadcasted_iota(jnp.int32, (B, PIECE), 1) >= B
    for i in range(NY):
        lanes = slice(i * PIECE, (i + 1) * PIECE)
        q = qc[lanes, :D]
        c = qc[lanes, D:]
        pieces = pieces_of(i)
        scores = [dot(keys[a : a + n, :], q, 1, 1) for a, n, _ in pieces]
        near = [scores[0][m * B : (m + 1) * B] for m in range(pieces[0][1] // B)]
        if i > 0:
            near[0] = jnp.where(second, -jnp.inf, near[0])
        if i < NY - 1:
            near[-1] = jnp.where(second, near[-1], -jnp.inf)
        scores[0] = jnp.concatenate(near, axis=0)
        top = functools.reduce(jnp.maximum, [jnp.max(s, axis=0, keepdims=True) for s in scores])
        total = []
        weighted = []
        for (a, n, r), s in zip(pieces, scores):
            e = jnp.exp2((s - top) * SCALE_LOG2E)
            g = dot(vals[a : a + n, :], c, 1, 1)
            raised[i, r : r + n, :] = e
            pgrads[i, r : r + n, :] = g
            total.append(jnp.sum(e, axis=0, keepdims=True))
            weighted.append(jnp.sum(e * g, axis=0, keepdims=True))
        stats[0:1, lanes] = top
        stats[1:2, lanes] = summed(total)
        stats[2:3, lanes] = summed(weighted)
    for n in range(COLS // B):
        cut = slice(n * B, (n + 1) * B)
        keys_t[:, cut] = keys[cut, :].T
        vals_t[:, cut] = vals[cut, :].T


def late_kernel(
    at_ref, from_1, from_3, from_7, qc, stats, top_ref, g_facing, g_other, edges, found, w5, s5, ew, es
):
    z = at_ref[1]
    odd = lax.rem(z, 2)
    edges[1 - odd] = from_1[B:]
    edges[odd] = jnp.where(by_three(z), from_3[HALF:], from_7[B:])
    first = lax.broadcasted_iota(jnp.int32, (B, PIECE), 1) < B
    for i in range(NY):
        lanes = slice(i * PIECE, (i + 1) * PIECE)
        q = qc[lanes, :D]
        c = qc[lanes, D:]
        scores = [dot(from_7[:B, :D], q, 1, 1)]
        pgrads = [dot(from_7[:B, D:], c, 1, 1)]
        side = {0: 0, NY - 1: 1}.get(i)
        if side is not None:
            score = dot(edges[side, :, :D], q, 1, 1)
            seen = first & (z > 0) if side == 0 else jnp.logical_not(first) & (z < NZ - 1)
            scores.append(jnp.where(seen, score, -jnp.inf))
            pgrads.append(dot(edges[side, :, D:], c, 1, 1))
        before = stats[0:1, lanes]
        top = functools.reduce(
            jnp.maximum, [before] + [jnp.max(s, axis=0, keepdims=True) for s in scores]
        )
        raised = [jnp.exp2((s - top) * SCALE_LOG2E) for s in scores]
        shrink = jnp.exp2((before - top) * SCALE_LOG2E)
        total = shrink * stats[1:2, lanes] + summed(
            [jnp.sum(e, axis=0, keepdims=True) for e in raised]
        )
        weighted = shrink * stats[2:3, lanes] + summed(
            [jnp.sum(e * g, axis=0, keepdims=True) for e, g in zip(raised, pgrads)]
        )
        inverse = 1.0 / total
        row_dot = inverse * weighted
        found[0:1, lanes] = shrink * inverse
        found[1:2, lanes] = row_dot
        probs = [e * inverse for e in raised]
        sgrads = [(p * (g - row_dot) * SCALE).astype(BF) for p, g in zip(probs, pgrads)]
        w5[:, lanes] = probs[0].astype(BF)
        s5[:, lanes] = sgrads[0]
        if side is not None:
            ew[side] = probs[1].astype(BF)
            es[side] = sgrads[1]
    top_ref[:B, :D] = dot(s5[...], qc[:, :D]).astype(BF)
    top_ref[:B, D:] = dot(w5[...], qc[:, D:]).astype(BF)

    def edge_grads(side):
        lanes = part_at(side * (NY - 1))
        key = dot(es[side], qc[lanes, :D]).astype(BF)
        value = dot(ew[side], qc[lanes, D:]).astype(BF)
        return key, value

    g_facing[:, :D], g_facing[:, D:] = edge_grads(1 - odd)
    key, value = edge_grads(odd)
    top_ref[B:, :D] = key
    top_ref[B:, D:] = value
    g_other[:, :D] = key
    g_other[:, D:] = value


def rest_kernel(
    at_ref, keys_t, vals_t, raised, pgrads, qc, from_7, edges, found, w5, s5, ew, es,
    og, g4, g3, g_own, g_one, g_two, grads,
):
    grads[...] = jnp.zeros_like(grads)
    five_k = from_7[:B, :D].T
    five_v = from_7[:B, D:].T
    for i in range(NY):
        lanes = slice(i * PIECE, (i + 1) * PIECE)
        q = qc[lanes, :D]
        c = qc[lanes, D:]
        ratio = found[0:1, lanes]
        row_dot = found[1:2, lanes]
        out_t = [dot(five_v, w5[:, lanes])]
        qg_t = [dot(five_k, s5[:, lanes])]
        side = {0: 0, NY - 1: 1}.get(i)
        if side is not None:
            out_t.append(dot(edges[side, :, D:].T, ew[side]))
            qg_t.append(dot(edges[side, :, :D].T, es[side]))
        for a, n, r in pieces_of(i):
            p = raised[i, r : r + n, :] * ratio
            w = p.astype(BF)
            s = (p * (pgrads[i, r : r + n, :] - row_dot) * SCALE).astype(BF)
            out_t.append(dot(vals_t[:, a : a + n], w))
            qg_t.append(dot(keys_t[:, a : a + n], s))
            grads[a : a + n, :D] += dot(s, q)
            grads[a : a + n, D:] += dot(w, c)
        og[lanes, :D] = summed(out_t).T.astype(BF)
        og[lanes, D:] = summed(qg_t).T.astype(BF)
    g_own[...] = grads[:AT1]
    g_one[...] = grads[AT1:AT2]
    g_two[...] = grads[AT2:AT3]
    g3[...] = grads[AT3 : AT3 + B]
    g4[...] = grads[AT3 + B :]


def spread_kernel(
    at_ref, back_ref, g4_ref, g3_ref, facing_ref, other_ref, s1_ref, s2_ref, s3_ref, keep_ref
):
    z = at_ref[1]
    twice = repeat_matrix(B // 4, 1)
    fourfold = repeat_matrix(B // 4, 2)

    def rows(d):
        return back_ref[part_at((z ^ d) & 3, SMALL), :]

    s1_ref[:B] = (g3_ref[...] + dot(fourfold, rows(1)) * 0.5).astype(BF)
    s1_ref[B:] = facing_ref[...]
    s2_ref[...] = (g4_ref[:HALF] + dot(twice, rows(2)) * ROOT_HALF).astype(BF)
    s3_ref[:HALF] = (g4_ref[HALF:] + dot(twice, rows(3)) * ROOT_HALF).astype(BF)
    s3_ref[HALF:] = other_ref[...]
    keep_ref[...] = dot(fourfold, rows(0)) * 0.5


def local_kernel(at_ref, own_ref, one_ref, two_ref, out_ref, *_):
    matrix = repeat_matrix(B, 1)
    for n in range(2):
        two = expand(matrix, two_ref[n * B : (n + 1) * B] * ROOT_HALF)
        for m in range(2):
            k = 2 * n + m
            one = one_ref[k * B : (k + 1) * B] + two[m * B : (m + 1) * B]
            cut = slice(k * PIECE, (k + 1) * PIECE)
            out_ref[cut] = own_ref[cut] + expand(matrix, one * ROOT_HALF)


def final_kernel(at_ref, own_ref, keep_ref, b1_ref, b2_ref, b3_ref, b7_ref, f0, f1, f2, f3, total):
    y = at_ref[0]
    z = at_ref[1]
    odd = lax.rem(z, 2)
    four = (b2_ref[...].astype(F32) + b3_ref[:HALF].astype(F32)) * ROOT_HALF
    up = keep_ref[...] + b1_ref[:B].astype(F32) + expand(repeat_matrix(HALF, 1), four)
    up *= ROOT_HALF * 0.5
    matrix = repeat_matrix(SMALL, 3)
    for n in range(NY):
        cut = slice(n * PIECE, (n + 1) * PIECE)
        total[cut] = own_ref[cut] + expand(matrix, up[n * SMALL : (n + 1) * SMALL])
    facing = part_at((1 - odd) * (PLANE // B - 1), B)
    total[facing, :] += b1_ref[B:].astype(F32)
    other = part_at(odd * (PLANE // B - 1), B)
    total[other, :] += jnp.where(by_three(z), b3_ref[HALF:], b7_ref[B:]).astype(F32)
    for d, ref in enumerate((f0, f1, f2, f3)):
        ref[...] = total[part_at(later(y, d)), :].astype(BF)


VMEM = pl.BlockSpec(memory_space=pltpu.VMEM)
SMEM = pl.BlockSpec(memory_space=pltpu.SMEM)
ANY = pl.BlockSpec(memory_space=pl.ANY)
HBM = pl.BlockSpec(memory_space=pltpu.HBM)


TOKEN = ((8, 128), F32)


def call(kernel, ins, outs, scratch=(), flops=10**6, source=VMEM, target=VMEM, after=(), vmem=8, alias=None):
    size = sum(a.size * a.dtype.itemsize for a in ins)
    size += sum(math.prod(s) * jnp.dtype(t).itemsize for s, t in outs)
    count = len(ins)

    def body(*refs):
        kernel(*refs[:count], *refs[count + len(after) :])

    return pl.pallas_call(
        body,
        out_shape=[jax.ShapeDtypeStruct(s, t) for s, t in outs],
        in_specs=[SMEM] + [source] * (count - 1) + [ANY] * len(after),
        out_specs=[target if s != TOKEN else VMEM for s in outs[: len(outs) - bool(alias)]]
        + [ANY] * bool(alias),
        scratch_shapes=list(scratch),
        input_output_aliases=alias or {},
        compiler_params=pltpu.CompilerParams(vmem_limit_bytes=vmem * 2**20),
        cost_estimate=pl.CostEstimate(flops=flops, bytes_accessed=size, transcendentals=0),
    )(*ins, *after)


def around_y(pieces):
    got = {0: pieces[0]}
    for d in Y_ORDER:
        got[d] = lax.ppermute(pieces[d], "y", [(i, (i + d) % NY) for i in range(NY)])
    return [got[d] for d in range(NY)]


def across_y(array):
    return lax.all_to_all(array, "y", split_axis=0, concat_axis=0, tiled=True)


def over_z(array, d):
    return lax.ppermute(array, "z", [(i, i ^ d) for i in range(NZ)])


def per_device(queries, keys, values, cotangent):
    at = jnp.stack([lax.axis_index("y"), lax.axis_index("z")]).astype(jnp.int32)
    piece = ((PIECE, 2 * D), BF)
    plane = ((PLANE, 2 * D), BF)
    level = ((B, 2 * D), BF)
    half = ((HALF, 2 * D), BF)
    tail = ((HALF + B, 2 * D), BF)
    double = ((2 * B, 2 * D), BF)
    wide = ((B, 2 * D), F32)
    sems = [pltpu.SemaphoreType.DMA((NY, 2))]
    kv = call(pack_kernel, [at, keys, values], [piece] * NY, scratch=sems, source=HBM)
    kv = around_y(kv)
    (qc_own,) = call(stack_kernel, [at, queries, cotangent], [plane], scratch=sems, source=HBM)
    qc = across_y(qc_own)
    kv, m1, m2, m3, own_tail = call(
        pool_kernel,
        [at, *kv],
        [plane, double, half, tail, tail],
        flops=POOL,
        after=[qc_own] if EARLY_STACK else [],
    )
    from_1, from_2, from_3 = over_z(m1, 1), over_z(m2, 2), over_z(m3, 3)
    (top,) = call(quad_kernel, [at, own_tail, from_1, from_2, from_3], [double])
    from_7 = over_z(top, 7)
    keys_t, vals_t, raised, pgrads, stats = call(
        early_kernel,
        [at, kv, from_1, from_2, from_3, qc],
        [((D, COLS), BF)] * 2 + [((NY, PAIR, PIECE), F32)] * 2 + [((8, PLANE), F32)],
        scratch=[pltpu.VMEM((COLS, D), BF)] * 2,
        flops=10**9,
        vmem=20,
    )
    g_top, g_facing, g_other, edges, found, w5, s5, ew, es = call(
        late_kernel,
        [at, from_1, from_3, from_7, qc, stats],
        [double, level, level, ((2, B, 2 * D), BF), ((8, PLANE), F32)]
        + [((B, PLANE), BF)] * 2
        + [((2, B, PIECE), BF)] * 2,
        flops=10**8,
    )
    og, g4, g3, g_own, g_one, g_two = call(
        rest_kernel,
        [at, keys_t, vals_t, raised, pgrads, qc, from_7, edges, found, w5, s5, ew, es],
        [plane, wide, wide]
        + [((PLANE, 2 * D), F32), ((PLANE // 2, 2 * D), F32), ((PLANE // 4, 2 * D), F32)],
        scratch=[pltpu.VMEM((COLS, 2 * D), F32)],
        flops=2 * 10**9,
        vmem=20,
    )
    back_7 = over_z(g_top, 7)
    s1, s2, s3, keep = call(
        spread_kernel,
        [at, back_7, g4, g3, g_facing, g_other],
        [double, half, tail, wide],
    )
    own, og = call(
        local_kernel,
        [at, g_own, g_one, g_two],
        [((PLANE, 2 * D), F32), plane],
        after=[og, keep],
        alias={4: 1},
    )
    og = across_y(og)
    back_1, back_2, back_3 = over_z(s1, 1), over_z(s2, 2), over_z(s3, 3)
    whole = ((PIECE, NY * D), BF)
    attended, grad_queries, token = call(
        unstack_kernel, [at, og], [whole] * 2 + [TOKEN], scratch=sems, target=HBM
    )
    final = call(
        final_kernel,
        [at, own, keep, back_1, back_2, back_3, back_7],
        [piece] * NY,
        scratch=[pltpu.VMEM((PLANE, 2 * D), F32)],
        flops=FINAL,
    )
    final = around_y(final)
    grad_keys, grad_values = call(
        unpack_kernel, [at, *final], [whole] * 2, scratch=sems, target=HBM, after=[token]
    )
    return attended, grad_queries, grad_keys, grad_values


def solution(mesh):
    seq, head, rep = mesh.devices.shape
    split = Mesh(mesh.devices.reshape(NZ, NY, head, rep), ("z", "y", "head", "rep"))
    spec = P(("rep", "z", "y"), "head")
    return jax.shard_map(
        per_device, mesh=split, in_specs=(spec,) * 4, out_specs=(spec,) * 4, check_vma=False
    )
```

```python
import functools
import math

import jax
import jax.numpy as jnp
from jax import lax
from jax.experimental import pallas as pl
from jax.experimental.pallas import tpu as pltpu
from jax.sharding import Mesh
from jax.sharding import PartitionSpec as P

D = 128
B = 128
HALF = B // 2
NY = 4
NZ = 8
PIECE = 2 * B
PLANE = NY * PIECE
SMALL = PIECE // 8
Y_ORDER = (1, 2, 3)
POOL = 5 * 10**9
FINAL = 5*10**9
EARLY_STACK = True
ROOT_HALF = 0.7071067811865476
SCALE = 1.0 / math.sqrt(D)
SCALE_LOG2E = SCALE * math.log2(math.e)
BF = jnp.bfloat16
F32 = jnp.float32

AT1 = PLANE
AT2 = AT1 + PLANE // 2
AT3 = AT2 + PLANE // 4
COLS = AT3 + 2 * B
PAIR = 8 * B


def dot(a, b, ca=1, cb=0):
    return lax.dot_general(a, b, (((ca,), (cb,)), ((), ())), preferred_element_type=F32)


def pair_sum(rows):
    r = lax.broadcasted_iota(jnp.int32, (rows, 2 * rows), 0)
    c = lax.broadcasted_iota(jnp.int32, (rows, 2 * rows), 1)
    return (lax.shift_right_logical(c, 1) == r).astype(F32).astype(BF)


def repeat_matrix(rows, log):
    r = lax.broadcasted_iota(jnp.int32, (rows << log, rows), 0)
    c = lax.broadcasted_iota(jnp.int32, (rows << log, rows), 1)
    return (lax.shift_right_logical(r, log) == c).astype(F32).astype(BF)


def pool(matrix, x):
    return (dot(matrix, x) * ROOT_HALF).astype(BF)


def expand(matrix, x):
    high = x.astype(BF)
    low = (x - high.astype(F32)).astype(BF)
    return dot(matrix, high) + dot(matrix, low)


def part_at(index, size=PIECE):
    return pl.ds(pl.multiple_of(index * size, size), size)


def head_at(index):
    return pl.ds(pl.multiple_of(index * D, D), D)


def later(y, d):
    return lax.rem(y + d, NY)


def earlier(y, d):
    return lax.rem(y - d + NY, NY)


def pack_kernel(left_hbm, right_hbm, *refs):
    outs, sems = refs[:NY], refs[-1]
    y = lax.axis_index("y")
    copies = [
        pltpu.make_async_copy(
            src.at[:, head_at(later(y, d))], outs[d].at[:, n * D : (n + 1) * D], sems.at[d, n]
        )
        for d in range(NY)
        for n, src in enumerate((left_hbm, right_hbm))
    ]
    for copy in copies:
        copy.start()
    for copy in copies:
        copy.wait()


def stack_kernel(left_hbm, right_hbm, out_ref, sems):
    copies = [
        pltpu.make_async_copy(
            src.at[:, h * D : (h + 1) * D],
            out_ref.at[h * PIECE : (h + 1) * PIECE, n * D : (n + 1) * D],
            sems.at[h, n],
        )
        for h in range(NY)
        for n, src in enumerate((left_hbm, right_hbm))
    ]
    for copy in copies:
        copy.start()
    for copy in copies:
        copy.wait()


def unstack_kernel(in_ref, left_hbm, right_hbm, token_ref, sems):
    token_ref[...] = jnp.zeros_like(token_ref)
    copies = [
        pltpu.make_async_copy(
            in_ref.at[h * PIECE : (h + 1) * PIECE, n * D : (n + 1) * D],
            dst.at[:, h * D : (h + 1) * D],
            sems.at[h, n],
        )
        for h in range(NY)
        for n, dst in enumerate((left_hbm, right_hbm))
    ]
    for copy in copies:
        copy.start()
    for copy in copies:
        copy.wait()


def unpack_kernel(*refs):
    pieces, left_hbm, right_hbm, sems = refs[:NY], refs[NY], refs[NY + 1], refs[-1]
    y = lax.axis_index("y")
    copies = [
        pltpu.make_async_copy(
            pieces[d].at[:, n * D : (n + 1) * D], dst.at[:, head_at(earlier(y, d))], sems.at[d, n]
        )
        for d in range(NY)
        for n, dst in enumerate((left_hbm, right_hbm))
    ]
    for copy in copies:
        copy.start()
    for copy in copies:
        copy.wait()


def pool_kernel(k0, k1, k2, k3, kv_ref, m1_ref, m2_ref, m3_ref, tail_ref):
    y = lax.axis_index("y")
    odd = lax.rem(lax.axis_index("z"), 2)
    for d, ref in enumerate((k0, k1, k2, k3)):
        kv_ref[part_at(earlier(y, d)), :] = ref[...]
    matrix = pair_sum(B)
    one = [pool(matrix, kv_ref[n * PIECE : (n + 1) * PIECE]) for n in range(4)]
    two = [pool(matrix, jnp.concatenate(one[n : n + 2], axis=0)) for n in (0, 2)]
    three = pool(matrix, jnp.concatenate(two, axis=0))
    four = pool(matrix[:HALF, :B], three)
    facing = kv_ref[part_at((1 - odd) * (PLANE // B - 1), B), :]
    other = kv_ref[part_at(odd * (PLANE // B - 1), B), :]
    m1_ref[:B] = three
    m1_ref[B:] = facing
    m2_ref[...] = four
    m3_ref[:HALF] = four
    m3_ref[HALF:] = other
    tail_ref[:HALF] = four
    tail_ref[HALF:] = other


def quad_kernel(tail_ref, three_1, four_2, four_3, top_ref):
    z = lax.axis_index("z")
    matrix = pair_sum(HALF)
    small = matrix[: B // 4, :HALF]
    fours = (tail_ref[:HALF], pool(matrix, three_1[:B]), four_2[...], four_3[:HALF])
    for d, four in enumerate(fours):
        top_ref[part_at((z ^ d) & 3, SMALL), :] = pool(small, four)
    top_ref[B:] = tail_ref[HALF:]


def by_three(z):
    return lax.rem(lax.shift_right_logical(z + 1, 1), 2) == 1


def pieces_of(i):
    start = max(0, i * PIECE - B)
    stop = min(PLANE, i * PIECE + 3 * B)
    return (
        (start, stop - start, start - (i * PIECE - B)),
        (AT1 + (i ^ 1) * B, B, 4 * B),
        (AT2 + ((i >> 1) ^ 1) * B, B, 5 * B),
        (AT3, 2 * B, 6 * B),
    )


def summed(values):
    return functools.reduce(jnp.add, values)


def early_kernel(
    kv, from_1, from_2, from_3, qc, keys_t, vals_t, raised, pgrads, stats, keys, vals
):
    matrix = pair_sum(B)
    one = [pool(matrix, kv[n * PIECE : (n + 1) * PIECE]) for n in range(4)]
    two = [pool(matrix, jnp.concatenate(one[n : n + 2], axis=0)) for n in (0, 2)]
    at = 0
    for part in (kv[...], *one, *two, from_1[:B], from_2[...], from_3[:HALF]):
        rows = part.shape[0]
        keys[at : at + rows, :] = part[:, :D]
        vals[at : at + rows, :] = part[:, D:]
        at += rows
    second = lax.broadcasted_iota(jnp.int32, (B, PIECE), 1) >= B
    for i in range(NY):
        lanes = slice(i * PIECE, (i + 1) * PIECE)
        q = qc[lanes, :D]
        c = qc[lanes, D:]
        pieces = pieces_of(i)
        scores = [dot(keys[a : a + n, :], q, 1, 1) for a, n, _ in pieces]
        near = [scores[0][m * B : (m + 1) * B] for m in range(pieces[0][1] // B)]
        if i > 0:
            near[0] = jnp.where(second, -jnp.inf, near[0])
        if i < NY - 1:
            near[-1] = jnp.where(second, near[-1], -jnp.inf)
        scores[0] = jnp.concatenate(near, axis=0)
        top = functools.reduce(jnp.maximum, [jnp.max(s, axis=0, keepdims=True) for s in scores])
        total = []
        weighted = []
        for (a, n, r), s in zip(pieces, scores):
            e = jnp.exp2((s - top) * SCALE_LOG2E)
            g = dot(vals[a : a + n, :], c, 1, 1)
            raised[i, r : r + n, :] = e
            pgrads[i, r : r + n, :] = g
            total.append(jnp.sum(e, axis=0, keepdims=True))
            weighted.append(jnp.sum(e * g, axis=0, keepdims=True))
        stats[0:1, lanes] = top
        stats[1:2, lanes] = summed(total)
        stats[2:3, lanes] = summed(weighted)
    for n in range(COLS // B):
        cut = slice(n * B, (n + 1) * B)
        keys_t[:, cut] = keys[cut, :].T
        vals_t[:, cut] = vals[cut, :].T


def late_kernel(
    from_1, from_3, from_7, qc, stats, top_ref, g_facing, g_other, edges, found, w5, s5, ew, es
):
    z = lax.axis_index("z")
    odd = lax.rem(z, 2)
    edges[1 - odd] = from_1[B:]
    edges[odd] = jnp.where(by_three(z), from_3[HALF:], from_7[B:])
    first = lax.broadcasted_iota(jnp.int32, (B, PIECE), 1) < B
    for i in range(NY):
        lanes = slice(i * PIECE, (i + 1) * PIECE)
        q = qc[lanes, :D]
        c = qc[lanes, D:]
        scores = [dot(from_7[:B, :D], q, 1, 1)]
        pgrads = [dot(from_7[:B, D:], c, 1, 1)]
        side = {0: 0, NY - 1: 1}.get(i)
        if side is not None:
            score = dot(edges[side, :, :D], q, 1, 1)
            seen = first & (z > 0) if side == 0 else jnp.logical_not(first) & (z < NZ - 1)
            scores.append(jnp.where(seen, score, -jnp.inf))
            pgrads.append(dot(edges[side, :, D:], c, 1, 1))
        before = stats[0:1, lanes]
        top = functools.reduce(
            jnp.maximum, [before] + [jnp.max(s, axis=0, keepdims=True) for s in scores]
        )
        raised = [jnp.exp2((s - top) * SCALE_LOG2E) for s in scores]
        shrink = jnp.exp2((before - top) * SCALE_LOG2E)
        total = shrink * stats[1:2, lanes] + summed(
            [jnp.sum(e, axis=0, keepdims=True) for e in raised]
        )
        weighted = shrink * stats[2:3, lanes] + summed(
            [jnp.sum(e * g, axis=0, keepdims=True) for e, g in zip(raised, pgrads)]
        )
        inverse = 1.0 / total
        row_dot = inverse * weighted
        found[0:1, lanes] = shrink * inverse
        found[1:2, lanes] = row_dot
        probs = [e * inverse for e in raised]
        sgrads = [(p * (g - row_dot) * SCALE).astype(BF) for p, g in zip(probs, pgrads)]
        w5[:, lanes] = probs[0].astype(BF)
        s5[:, lanes] = sgrads[0]
        if side is not None:
            ew[side] = probs[1].astype(BF)
            es[side] = sgrads[1]
    top_ref[:B, :D] = dot(s5[...], qc[:, :D]).astype(BF)
    top_ref[:B, D:] = dot(w5[...], qc[:, D:]).astype(BF)

    def edge_grads(side):
        lanes = part_at(side * (NY - 1))
        key = dot(es[side], qc[lanes, :D]).astype(BF)
        value = dot(ew[side], qc[lanes, D:]).astype(BF)
        return key, value

    g_facing[:, :D], g_facing[:, D:] = edge_grads(1 - odd)
    key, value = edge_grads(odd)
    top_ref[B:, :D] = key
    top_ref[B:, D:] = value
    g_other[:, :D] = key
    g_other[:, D:] = value


def rest_kernel(
    keys_t, vals_t, raised, pgrads, qc, from_7, edges, found, w5, s5, ew, es,
    og, g4, g3, g_own, g_one, g_two, grads,
):
    grads[...] = jnp.zeros_like(grads)
    five_k = from_7[:B, :D].T
    five_v = from_7[:B, D:].T
    for i in range(NY):
        lanes = slice(i * PIECE, (i + 1) * PIECE)
        q = qc[lanes, :D]
        c = qc[lanes, D:]
        ratio = found[0:1, lanes]
        row_dot = found[1:2, lanes]
        out_t = [dot(five_v, w5[:, lanes])]
        qg_t = [dot(five_k, s5[:, lanes])]
        side = {0: 0, NY - 1: 1}.get(i)
        if side is not None:
            out_t.append(dot(edges[side, :, D:].T, ew[side]))
            qg_t.append(dot(edges[side, :, :D].T, es[side]))
        for a, n, r in pieces_of(i):
            p = raised[i, r : r + n, :] * ratio
            w = p.astype(BF)
            s = (p * (pgrads[i, r : r + n, :] - row_dot) * SCALE).astype(BF)
            out_t.append(dot(vals_t[:, a : a + n], w))
            qg_t.append(dot(keys_t[:, a : a + n], s))
            grads[a : a + n, :D] += dot(s, q)
            grads[a : a + n, D:] += dot(w, c)
        og[lanes, :D] = summed(out_t).T.astype(BF)
        og[lanes, D:] = summed(qg_t).T.astype(BF)
    g_own[...] = grads[:AT1]
    g_one[...] = grads[AT1:AT2]
    g_two[...] = grads[AT2:AT3]
    g3[...] = grads[AT3 : AT3 + B]
    g4[...] = grads[AT3 + B :]


def spread_kernel(
    back_ref, g4_ref, g3_ref, facing_ref, other_ref, s1_ref, s2_ref, s3_ref, keep_ref
):
    z = lax.axis_index("z")
    twice = repeat_matrix(B // 4, 1)
    fourfold = repeat_matrix(B // 4, 2)

    def rows(d):
        return back_ref[part_at((z ^ d) & 3, SMALL), :]

    s1_ref[:B] = (g3_ref[...] + dot(fourfold, rows(1)) * 0.5).astype(BF)
    s1_ref[B:] = facing_ref[...]
    s2_ref[...] = (g4_ref[:HALF] + dot(twice, rows(2)) * ROOT_HALF).astype(BF)
    s3_ref[:HALF] = (g4_ref[HALF:] + dot(twice, rows(3)) * ROOT_HALF).astype(BF)
    s3_ref[HALF:] = other_ref[...]
    keep_ref[...] = dot(fourfold, rows(0)) * 0.5


def local_kernel(own_ref, one_ref, two_ref, out_ref, *_):
    matrix = repeat_matrix(B, 1)
    for n in range(2):
        two = expand(matrix, two_ref[n * B : (n + 1) * B] * ROOT_HALF)
        for m in range(2):
            k = 2 * n + m
            one = one_ref[k * B : (k + 1) * B] + two[m * B : (m + 1) * B]
            cut = slice(k * PIECE, (k + 1) * PIECE)
            out_ref[cut] = own_ref[cut] + expand(matrix, one * ROOT_HALF)


def final_kernel(own_ref, keep_ref, b1_ref, b2_ref, b3_ref, b7_ref, f0, f1, f2, f3, total):
    y = lax.axis_index("y")
    z = lax.axis_index("z")
    odd = lax.rem(z, 2)
    four = (b2_ref[...].astype(F32) + b3_ref[:HALF].astype(F32)) * ROOT_HALF
    up = keep_ref[...] + b1_ref[:B].astype(F32) + expand(repeat_matrix(HALF, 1), four)
    up *= ROOT_HALF * 0.5
    matrix = repeat_matrix(SMALL, 3)
    for n in range(NY):
        cut = slice(n * PIECE, (n + 1) * PIECE)
        total[cut] = own_ref[cut] + expand(matrix, up[n * SMALL : (n + 1) * SMALL])
    facing = part_at((1 - odd) * (PLANE // B - 1), B)
    total[facing, :] += b1_ref[B:].astype(F32)
    other = part_at(odd * (PLANE // B - 1), B)
    total[other, :] += jnp.where(by_three(z), b3_ref[HALF:], b7_ref[B:]).astype(F32)
    for d, ref in enumerate((f0, f1, f2, f3)):
        ref[...] = total[part_at(later(y, d)), :].astype(BF)


VMEM = pl.BlockSpec(memory_space=pltpu.VMEM)
ANY = pl.BlockSpec(memory_space=pl.ANY)
HBM = pl.BlockSpec(memory_space=pltpu.HBM)


TOKEN = ((8, 128), F32)


def call(kernel, ins, outs, scratch=(), flops=10**6, source=VMEM, target=VMEM, after=(), vmem=8, alias=None):
    size = sum(a.size * a.dtype.itemsize for a in ins)
    size += sum(math.prod(s) * jnp.dtype(t).itemsize for s, t in outs)
    count = len(ins)

    def body(*refs):
        kernel(*refs[:count], *refs[count + len(after) :])

    return pl.pallas_call(
        body,
        out_shape=[jax.ShapeDtypeStruct(s, t) for s, t in outs],
        in_specs=[source] * count + [ANY] * len(after),
        out_specs=[target if s != TOKEN else VMEM for s in outs[: len(outs) - bool(alias)]]
        + [ANY] * bool(alias),
        scratch_shapes=list(scratch),
        input_output_aliases=alias or {},
        compiler_params=pltpu.CompilerParams(vmem_limit_bytes=vmem * 2**20),
        cost_estimate=pl.CostEstimate(flops=flops, bytes_accessed=size, transcendentals=0),
    )(*ins, *after)


def around_y(pieces):
    got = {0: pieces[0]}
    for d in Y_ORDER:
        got[d] = lax.ppermute(pieces[d], "y", [(i, (i + d) % NY) for i in range(NY)])
    return [got[d] for d in range(NY)]


def across_y(array):
    return lax.all_to_all(array, "y", split_axis=0, concat_axis=0, tiled=True)


def over_z(array, d):
    return lax.ppermute(array, "z", [(i, i ^ d) for i in range(NZ)])


def per_device(queries, keys, values, cotangent):
    piece = ((PIECE, 2 * D), BF)
    plane = ((PLANE, 2 * D), BF)
    level = ((B, 2 * D), BF)
    half = ((HALF, 2 * D), BF)
    tail = ((HALF + B, 2 * D), BF)
    double = ((2 * B, 2 * D), BF)
    wide = ((B, 2 * D), F32)
    sems = [pltpu.SemaphoreType.DMA((NY, 2))]
    kv = call(pack_kernel, [keys, values], [piece] * NY, scratch=sems, source=HBM, flops=5 * 10**9)
    kv = around_y(kv)
    (qc_own,) = call(stack_kernel, [queries, cotangent], [plane], scratch=sems, source=HBM)
    qc = across_y(qc_own)
    kv, m1, m2, m3, own_tail = call(
        pool_kernel,
        [*kv],
        [plane, double, half, tail, tail],
        flops=POOL,
        after=[qc_own] if EARLY_STACK else [],
    )
    from_1, from_2, from_3 = over_z(m1, 1), over_z(m2, 2), over_z(m3, 3)
    (top,) = call(quad_kernel, [own_tail, from_1, from_2, from_3], [double])
    from_7 = over_z(top, 7)
    keys_t, vals_t, raised, pgrads, stats = call(
        early_kernel,
        [kv, from_1, from_2, from_3, qc],
        [((D, COLS), BF)] * 2 + [((NY, PAIR, PIECE), F32)] * 2 + [((8, PLANE), F32)],
        scratch=[pltpu.VMEM((COLS, D), BF)] * 2,
        flops=10**9,
        vmem=20,
    )
    g_top, g_facing, g_other, edges, found, w5, s5, ew, es = call(
        late_kernel,
        [from_1, from_3, from_7, qc, stats],
        [double, level, level, ((2, B, 2 * D), BF), ((8, PLANE), F32)]
        + [((B, PLANE), BF)] * 2
        + [((2, B, PIECE), BF)] * 2,
        flops=10**8,
    )
    og, g4, g3, g_own, g_one, g_two = call(
        rest_kernel,
        [keys_t, vals_t, raised, pgrads, qc, from_7, edges, found, w5, s5, ew, es],
        [plane, wide, wide]
        + [((PLANE, 2 * D), F32), ((PLANE // 2, 2 * D), F32), ((PLANE // 4, 2 * D), F32)],
        scratch=[pltpu.VMEM((COLS, 2 * D), F32)],
        flops=2 * 10**9,
        vmem=20,
    )
    back_7 = over_z(g_top, 7)
    s1, s2, s3, keep = call(
        spread_kernel,
        [back_7, g4, g3, g_facing, g_other],
        [double, half, tail, wide],
    )
    own, og = call(
        local_kernel,
        [g_own, g_one, g_two],
        [((PLANE, 2 * D), F32), plane],
        after=[og, keep],
        alias={3: 1},
    )
    og = across_y(og)
    back_1, back_2, back_3 = over_z(s1, 1), over_z(s2, 2), over_z(s3, 3)
    whole = ((PIECE, NY * D), BF)
    attended, grad_queries, token = call(
        unstack_kernel, [og], [whole] * 2 + [TOKEN], scratch=sems, target=HBM
    )
    final = call(
        final_kernel,
        [own, keep, back_1, back_2, back_3, back_7],
        [piece] * NY,
        scratch=[pltpu.VMEM((PLANE, 2 * D), F32)],
        flops=FINAL,
    )
    final = around_y(final)
    grad_keys, grad_values = call(
        unpack_kernel, [*final], [whole] * 2, scratch=sems, target=HBM, after=[token]
    )
    return attended, grad_queries, grad_keys, grad_values


def solution(mesh):
    seq, head, rep = mesh.devices.shape
    split = Mesh(mesh.devices.reshape(NZ, NY, head, rep), ("z", "y", "head", "rep"))
    spec = P(("rep", "z", "y"), "head")
    return jax.shard_map(
        per_device, mesh=split, in_specs=(spec,) * 4, out_specs=(spec,) * 4, check_vma=False
    )
```

```python
import functools
import math

import jax
import jax.numpy as jnp
from jax import lax
from jax.experimental import pallas as pl
from jax.experimental.pallas import tpu as pltpu
from jax.sharding import Mesh
from jax.sharding import PartitionSpec as P

D = 128
B = 128
HALF = B // 2
NY = 4
NZ = 8
PIECE = 2 * B
PLANE = NY * PIECE
SMALL = PIECE // 8
Y_ORDER = (1, 2, 3)
POOL = 5 * 10**9
FIRST = 5 * 10**9
FINAL = 5*10**9
EARLY_STACK = True
ROOT_HALF = 0.7071067811865476
SCALE = 1.0 / math.sqrt(D)
SCALE_LOG2E = SCALE * math.log2(math.e)
BF = jnp.bfloat16
F32 = jnp.float32

AT1 = PLANE
AT2 = AT1 + PLANE // 2
AT3 = AT2 + PLANE // 4
COLS = AT3 + 2 * B
PAIR = 8 * B


def dot(a, b, ca=1, cb=0):
    return lax.dot_general(a, b, (((ca,), (cb,)), ((), ())), preferred_element_type=F32)


def pair_sum(rows):
    r = lax.broadcasted_iota(jnp.int32, (rows, 2 * rows), 0)
    c = lax.broadcasted_iota(jnp.int32, (rows, 2 * rows), 1)
    return (lax.shift_right_logical(c, 1) == r).astype(F32).astype(BF)


def repeat_matrix(rows, log):
    r = lax.broadcasted_iota(jnp.int32, (rows << log, rows), 0)
    c = lax.broadcasted_iota(jnp.int32, (rows << log, rows), 1)
    return (lax.shift_right_logical(r, log) == c).astype(F32).astype(BF)


def pool(matrix, x):
    return (dot(matrix, x) * ROOT_HALF).astype(BF)


def expand(matrix, x):
    high = x.astype(BF)
    low = (x - high.astype(F32)).astype(BF)
    return dot(matrix, high) + dot(matrix, low)


def part_at(index, size=PIECE):
    return pl.ds(pl.multiple_of(index * size, size), size)


def head_at(index):
    return pl.ds(pl.multiple_of(index * D, D), D)


def later(y, d):
    return lax.rem(y + d, NY)


def earlier(y, d):
    return lax.rem(y - d + NY, NY)


def first_kernel(token_ref):
    token_ref[...] = jnp.zeros_like(token_ref)


def pack_kernel(left_hbm, right_hbm, *refs):
    outs, sems = refs[:NY], refs[-1]
    y = lax.axis_index("y")
    copies = [
        pltpu.make_async_copy(
            src.at[:, head_at(later(y, d))], outs[d].at[:, n * D : (n + 1) * D], sems.at[d, n]
        )
        for d in range(NY)
        for n, src in enumerate((left_hbm, right_hbm))
    ]
    for copy in copies:
        copy.start()
    for copy in copies:
        copy.wait()


def stack_kernel(left_hbm, right_hbm, out_ref, sems):
    copies = [
        pltpu.make_async_copy(
            src.at[:, h * D : (h + 1) * D],
            out_ref.at[h * PIECE : (h + 1) * PIECE, n * D : (n + 1) * D],
            sems.at[h, n],
        )
        for h in range(NY)
        for n, src in enumerate((left_hbm, right_hbm))
    ]
    for copy in copies:
        copy.start()
    for copy in copies:
        copy.wait()


def unstack_kernel(in_ref, left_hbm, right_hbm, token_ref, sems):
    token_ref[...] = jnp.zeros_like(token_ref)
    copies = [
        pltpu.make_async_copy(
            in_ref.at[h * PIECE : (h + 1) * PIECE, n * D : (n + 1) * D],
            dst.at[:, h * D : (h + 1) * D],
            sems.at[h, n],
        )
        for h in range(NY)
        for n, dst in enumerate((left_hbm, right_hbm))
    ]
    for copy in copies:
        copy.start()
    for copy in copies:
        copy.wait()


def unpack_kernel(*refs):
    pieces, left_hbm, right_hbm, sems = refs[:NY], refs[NY], refs[NY + 1], refs[-1]
    y = lax.axis_index("y")
    copies = [
        pltpu.make_async_copy(
            pieces[d].at[:, n * D : (n + 1) * D], dst.at[:, head_at(earlier(y, d))], sems.at[d, n]
        )
        for d in range(NY)
        for n, dst in enumerate((left_hbm, right_hbm))
    ]
    for copy in copies:
        copy.start()
    for copy in copies:
        copy.wait()


def pool_kernel(k0, k1, k2, k3, kv_ref, m1_ref, m2_ref, m3_ref, tail_ref):
    y = lax.axis_index("y")
    odd = lax.rem(lax.axis_index("z"), 2)
    for d, ref in enumerate((k0, k1, k2, k3)):
        kv_ref[part_at(earlier(y, d)), :] = ref[...]
    matrix = pair_sum(B)
    one = [pool(matrix, kv_ref[n * PIECE : (n + 1) * PIECE]) for n in range(4)]
    two = [pool(matrix, jnp.concatenate(one[n : n + 2], axis=0)) for n in (0, 2)]
    three = pool(matrix, jnp.concatenate(two, axis=0))
    four = pool(matrix[:HALF, :B], three)
    facing = kv_ref[part_at((1 - odd) * (PLANE // B - 1), B), :]
    other = kv_ref[part_at(odd * (PLANE // B - 1), B), :]
    m1_ref[:B] = three
    m1_ref[B:] = facing
    m2_ref[...] = four
    m3_ref[:HALF] = four
    m3_ref[HALF:] = other
    tail_ref[:HALF] = four
    tail_ref[HALF:] = other


def quad_kernel(tail_ref, three_1, four_2, four_3, top_ref):
    z = lax.axis_index("z")
    matrix = pair_sum(HALF)
    small = matrix[: B // 4, :HALF]
    fours = (tail_ref[:HALF], pool(matrix, three_1[:B]), four_2[...], four_3[:HALF])
    for d, four in enumerate(fours):
        top_ref[part_at((z ^ d) & 3, SMALL), :] = pool(small, four)
    top_ref[B:] = tail_ref[HALF:]


def by_three(z):
    return lax.rem(lax.shift_right_logical(z + 1, 1), 2) == 1


def pieces_of(i):
    start = max(0, i * PIECE - B)
    stop = min(PLANE, i * PIECE + 3 * B)
    return (
        (start, stop - start, start - (i * PIECE - B)),
        (AT1 + (i ^ 1) * B, B, 4 * B),
        (AT2 + ((i >> 1) ^ 1) * B, B, 5 * B),
        (AT3, 2 * B, 6 * B),
    )


def summed(values):
    return functools.reduce(jnp.add, values)


def early_kernel(
    kv, from_1, from_2, from_3, qc, keys_t, vals_t, raised, pgrads, stats, keys, vals
):
    matrix = pair_sum(B)
    one = [pool(matrix, kv[n * PIECE : (n + 1) * PIECE]) for n in range(4)]
    two = [pool(matrix, jnp.concatenate(one[n : n + 2], axis=0)) for n in (0, 2)]
    at = 0
    for part in (kv[...], *one, *two, from_1[:B], from_2[...], from_3[:HALF]):
        rows = part.shape[0]
        keys[at : at + rows, :] = part[:, :D]
        vals[at : at + rows, :] = part[:, D:]
        at += rows
    second = lax.broadcasted_iota(jnp.int32, (B, PIECE), 1) >= B
    for i in range(NY):
        lanes = slice(i * PIECE, (i + 1) * PIECE)
        q = qc[lanes, :D]
        c = qc[lanes, D:]
        pieces = pieces_of(i)
        scores = [dot(keys[a : a + n, :], q, 1, 1) for a, n, _ in pieces]
        near = [scores[0][m * B : (m + 1) * B] for m in range(pieces[0][1] // B)]
        if i > 0:
            near[0] = jnp.where(second, -jnp.inf, near[0])
        if i < NY - 1:
            near[-1] = jnp.where(second, near[-1], -jnp.inf)
        scores[0] = jnp.concatenate(near, axis=0)
        top = functools.reduce(jnp.maximum, [jnp.max(s, axis=0, keepdims=True) for s in scores])
        total = []
        weighted = []
        for (a, n, r), s in zip(pieces, scores):
            e = jnp.exp2((s - top) * SCALE_LOG2E)
            g = dot(vals[a : a + n, :], c, 1, 1)
            raised[i, r : r + n, :] = e
            pgrads[i, r : r + n, :] = g
            total.append(jnp.sum(e, axis=0, keepdims=True))
            weighted.append(jnp.sum(e * g, axis=0, keepdims=True))
        stats[0:1, lanes] = top
        stats[1:2, lanes] = summed(total)
        stats[2:3, lanes] = summed(weighted)
    for n in range(COLS // B):
        cut = slice(n * B, (n + 1) * B)
        keys_t[:, cut] = keys[cut, :].T
        vals_t[:, cut] = vals[cut, :].T


def late_kernel(
    from_1, from_3, from_7, qc, stats, top_ref, g_facing, g_other, edges, found, w5, s5, ew, es
):
    z = lax.axis_index("z")
    odd = lax.rem(z, 2)
    edges[1 - odd] = from_1[B:]
    edges[odd] = jnp.where(by_three(z), from_3[HALF:], from_7[B:])
    first = lax.broadcasted_iota(jnp.int32, (B, PIECE), 1) < B
    for i in range(NY):
        lanes = slice(i * PIECE, (i + 1) * PIECE)
        q = qc[lanes, :D]
        c = qc[lanes, D:]
        scores = [dot(from_7[:B, :D], q, 1, 1)]
        pgrads = [dot(from_7[:B, D:], c, 1, 1)]
        side = {0: 0, NY - 1: 1}.get(i)
        if side is not None:
            score = dot(edges[side, :, :D], q, 1, 1)
            seen = first & (z > 0) if side == 0 else jnp.logical_not(first) & (z < NZ - 1)
            scores.append(jnp.where(seen, score, -jnp.inf))
            pgrads.append(dot(edges[side, :, D:], c, 1, 1))
        before = stats[0:1, lanes]
        top = functools.reduce(
            jnp.maximum, [before] + [jnp.max(s, axis=0, keepdims=True) for s in scores]
        )
        raised = [jnp.exp2((s - top) * SCALE_LOG2E) for s in scores]
        shrink = jnp.exp2((before - top) * SCALE_LOG2E)
        total = shrink * stats[1:2, lanes] + summed(
            [jnp.sum(e, axis=0, keepdims=True) for e in raised]
        )
        weighted = shrink * stats[2:3, lanes] + summed(
            [jnp.sum(e * g, axis=0, keepdims=True) for e, g in zip(raised, pgrads)]
        )
        inverse = 1.0 / total
        row_dot = inverse * weighted
        found[0:1, lanes] = shrink * inverse
        found[1:2, lanes] = row_dot
        probs = [e * inverse for e in raised]
        sgrads = [(p * (g - row_dot) * SCALE).astype(BF) for p, g in zip(probs, pgrads)]
        w5[:, lanes] = probs[0].astype(BF)
        s5[:, lanes] = sgrads[0]
        if side is not None:
            ew[side] = probs[1].astype(BF)
            es[side] = sgrads[1]
    top_ref[:B, :D] = dot(s5[...], qc[:, :D]).astype(BF)
    top_ref[:B, D:] = dot(w5[...], qc[:, D:]).astype(BF)

    def edge_grads(side):
        lanes = part_at(side * (NY - 1))
        key = dot(es[side], qc[lanes, :D]).astype(BF)
        value = dot(ew[side], qc[lanes, D:]).astype(BF)
        return key, value

    g_facing[:, :D], g_facing[:, D:] = edge_grads(1 - odd)
    key, value = edge_grads(odd)
    top_ref[B:, :D] = key
    top_ref[B:, D:] = value
    g_other[:, :D] = key
    g_other[:, D:] = value


def rest_kernel(
    keys_t, vals_t, raised, pgrads, qc, from_7, edges, found, w5, s5, ew, es,
    og, g4, g3, g_own, g_one, g_two, grads,
):
    grads[...] = jnp.zeros_like(grads)
    five_k = from_7[:B, :D].T
    five_v = from_7[:B, D:].T
    for i in range(NY):
        lanes = slice(i * PIECE, (i + 1) * PIECE)
        q = qc[lanes, :D]
        c = qc[lanes, D:]
        ratio = found[0:1, lanes]
        row_dot = found[1:2, lanes]
        out_t = [dot(five_v, w5[:, lanes])]
        qg_t = [dot(five_k, s5[:, lanes])]
        side = {0: 0, NY - 1: 1}.get(i)
        if side is not None:
            out_t.append(dot(edges[side, :, D:].T, ew[side]))
            qg_t.append(dot(edges[side, :, :D].T, es[side]))
        for a, n, r in pieces_of(i):
            p = raised[i, r : r + n, :] * ratio
            w = p.astype(BF)
            s = (p * (pgrads[i, r : r + n, :] - row_dot) * SCALE).astype(BF)
            out_t.append(dot(vals_t[:, a : a + n], w))
            qg_t.append(dot(keys_t[:, a : a + n], s))
            grads[a : a + n, :D] += dot(s, q)
            grads[a : a + n, D:] += dot(w, c)
        og[lanes, :D] = summed(out_t).T.astype(BF)
        og[lanes, D:] = summed(qg_t).T.astype(BF)
    g_own[...] = grads[:AT1]
    g_one[...] = grads[AT1:AT2]
    g_two[...] = grads[AT2:AT3]
    g3[...] = grads[AT3 : AT3 + B]
    g4[...] = grads[AT3 + B :]


def spread_kernel(
    back_ref, g4_ref, g3_ref, facing_ref, other_ref, s1_ref, s2_ref, s3_ref, keep_ref
):
    z = lax.axis_index("z")
    twice = repeat_matrix(B // 4, 1)
    fourfold = repeat_matrix(B // 4, 2)

    def rows(d):
        return back_ref[part_at((z ^ d) & 3, SMALL), :]

    s1_ref[:B] = (g3_ref[...] + dot(fourfold, rows(1)) * 0.5).astype(BF)
    s1_ref[B:] = facing_ref[...]
    s2_ref[...] = (g4_ref[:HALF] + dot(twice, rows(2)) * ROOT_HALF).astype(BF)
    s3_ref[:HALF] = (g4_ref[HALF:] + dot(twice, rows(3)) * ROOT_HALF).astype(BF)
    s3_ref[HALF:] = other_ref[...]
    keep_ref[...] = dot(fourfold, rows(0)) * 0.5


def local_kernel(own_ref, one_ref, two_ref, out_ref, *_):
    matrix = repeat_matrix(B, 1)
    for n in range(2):
        two = expand(matrix, two_ref[n * B : (n + 1) * B] * ROOT_HALF)
        for m in range(2):
            k = 2 * n + m
            one = one_ref[k * B : (k + 1) * B] + two[m * B : (m + 1) * B]
            cut = slice(k * PIECE, (k + 1) * PIECE)
            out_ref[cut] = own_ref[cut] + expand(matrix, one * ROOT_HALF)


def final_kernel(own_ref, keep_ref, b1_ref, b2_ref, b3_ref, b7_ref, f0, f1, f2, f3, total):
    y = lax.axis_index("y")
    z = lax.axis_index("z")
    odd = lax.rem(z, 2)
    four = (b2_ref[...].astype(F32) + b3_ref[:HALF].astype(F32)) * ROOT_HALF
    up = keep_ref[...] + b1_ref[:B].astype(F32) + expand(repeat_matrix(HALF, 1), four)
    up *= ROOT_HALF * 0.5
    matrix = repeat_matrix(SMALL, 3)
    for n in range(NY):
        cut = slice(n * PIECE, (n + 1) * PIECE)
        total[cut] = own_ref[cut] + expand(matrix, up[n * SMALL : (n + 1) * SMALL])
    facing = part_at((1 - odd) * (PLANE // B - 1), B)
    total[facing, :] += b1_ref[B:].astype(F32)
    other = part_at(odd * (PLANE // B - 1), B)
    total[other, :] += jnp.where(by_three(z), b3_ref[HALF:], b7_ref[B:]).astype(F32)
    for d, ref in enumerate((f0, f1, f2, f3)):
        ref[...] = total[part_at(later(y, d)), :].astype(BF)


VMEM = pl.BlockSpec(memory_space=pltpu.VMEM)
ANY = pl.BlockSpec(memory_space=pl.ANY)
HBM = pl.BlockSpec(memory_space=pltpu.HBM)


TOKEN = ((8, 128), F32)


def call(kernel, ins, outs, scratch=(), flops=10**6, source=VMEM, target=VMEM, after=(), vmem=8, alias=None):
    size = sum(a.size * a.dtype.itemsize for a in ins)
    size += sum(math.prod(s) * jnp.dtype(t).itemsize for s, t in outs)
    count = len(ins)

    def body(*refs):
        kernel(*refs[:count], *refs[count + len(after) :])

    return pl.pallas_call(
        body,
        out_shape=[jax.ShapeDtypeStruct(s, t) for s, t in outs],
        in_specs=[source] * count + [ANY] * len(after),
        out_specs=[target if s != TOKEN else VMEM for s in outs[: len(outs) - bool(alias)]]
        + [ANY] * bool(alias),
        scratch_shapes=list(scratch),
        input_output_aliases=alias or {},
        compiler_params=pltpu.CompilerParams(vmem_limit_bytes=vmem * 2**20),
        cost_estimate=pl.CostEstimate(flops=flops, bytes_accessed=size, transcendentals=0),
    )(*ins, *after)


def around_y(pieces):
    got = {0: pieces[0]}
    for d in Y_ORDER:
        got[d] = lax.ppermute(pieces[d], "y", [(i, (i + d) % NY) for i in range(NY)])
    return [got[d] for d in range(NY)]


def across_y(array):
    return lax.all_to_all(array, "y", split_axis=0, concat_axis=0, tiled=True)


def over_z(array, d):
    return lax.ppermute(array, "z", [(i, i ^ d) for i in range(NZ)])


def per_device(queries, keys, values, cotangent):
    piece = ((PIECE, 2 * D), BF)
    plane = ((PLANE, 2 * D), BF)
    level = ((B, 2 * D), BF)
    half = ((HALF, 2 * D), BF)
    tail = ((HALF + B, 2 * D), BF)
    double = ((2 * B, 2 * D), BF)
    wide = ((B, 2 * D), F32)
    sems = [pltpu.SemaphoreType.DMA((NY, 2))]
    (token,) = call(first_kernel, [], [TOKEN], flops=FIRST)
    kv = call(
        pack_kernel, [keys, values], [piece] * NY, scratch=sems, source=HBM, flops=5 * 10**9, after=[token]
    )
    kv = around_y(kv)
    (qc_own,) = call(stack_kernel, [queries, cotangent], [plane], scratch=sems, source=HBM)
    qc = across_y(qc_own)
    kv, m1, m2, m3, own_tail = call(
        pool_kernel,
        [*kv],
        [plane, double, half, tail, tail],
        flops=POOL,
        after=[qc_own] if EARLY_STACK else [],
    )
    from_1, from_2, from_3 = over_z(m1, 1), over_z(m2, 2), over_z(m3, 3)
    (top,) = call(quad_kernel, [own_tail, from_1, from_2, from_3], [double])
    from_7 = over_z(top, 7)
    keys_t, vals_t, raised, pgrads, stats = call(
        early_kernel,
        [kv, from_1, from_2, from_3, qc],
        [((D, COLS), BF)] * 2 + [((NY, PAIR, PIECE), F32)] * 2 + [((8, PLANE), F32)],
        scratch=[pltpu.VMEM((COLS, D), BF)] * 2,
        flops=10**9,
        vmem=20,
    )
    g_top, g_facing, g_other, edges, found, w5, s5, ew, es = call(
        late_kernel,
        [from_1, from_3, from_7, qc, stats],
        [double, level, level, ((2, B, 2 * D), BF), ((8, PLANE), F32)]
        + [((B, PLANE), BF)] * 2
        + [((2, B, PIECE), BF)] * 2,
        flops=10**8,
    )
    og, g4, g3, g_own, g_one, g_two = call(
        rest_kernel,
        [keys_t, vals_t, raised, pgrads, qc, from_7, edges, found, w5, s5, ew, es],
        [plane, wide, wide]
        + [((PLANE, 2 * D), F32), ((PLANE // 2, 2 * D), F32), ((PLANE // 4, 2 * D), F32)],
        scratch=[pltpu.VMEM((COLS, 2 * D), F32)],
        flops=2 * 10**9,
        vmem=20,
    )
    back_7 = over_z(g_top, 7)
    s1, s2, s3, keep = call(
        spread_kernel,
        [back_7, g4, g3, g_facing, g_other],
        [double, half, tail, wide],
    )
    own, og = call(
        local_kernel,
        [g_own, g_one, g_two],
        [((PLANE, 2 * D), F32), plane],
        after=[og, keep],
        alias={3: 1},
    )
    og = across_y(og)
    back_1, back_2, back_3 = over_z(s1, 1), over_z(s2, 2), over_z(s3, 3)
    whole = ((PIECE, NY * D), BF)
    attended, grad_queries, token = call(
        unstack_kernel, [og], [whole] * 2 + [TOKEN], scratch=sems, target=HBM
    )
    final = call(
        final_kernel,
        [own, keep, back_1, back_2, back_3, back_7],
        [piece] * NY,
        scratch=[pltpu.VMEM((PLANE, 2 * D), F32)],
        flops=FINAL,
    )
    final = around_y(final)
    grad_keys, grad_values = call(
        unpack_kernel, [*final], [whole] * 2, scratch=sems, target=HBM, after=[token]
    )
    return attended, grad_queries, grad_keys, grad_values


def solution(mesh):
    seq, head, rep = mesh.devices.shape
    split = Mesh(mesh.devices.reshape(NZ, NY, head, rep), ("z", "y", "head", "rep"))
    spec = P(("rep", "z", "y"), "head")
    return jax.shard_map(
        per_device, mesh=split, in_specs=(spec,) * 4, out_specs=(spec,) * 4, check_vma=False
    )
```

```python
import functools
import math

import jax
import jax.numpy as jnp
from jax import lax
from jax.experimental import pallas as pl
from jax.experimental.pallas import tpu as pltpu
from jax.sharding import Mesh
from jax.sharding import PartitionSpec as P

D = 128
B = 128
HALF = B // 2
NY = 4
NZ = 8
PIECE = 2 * B
PLANE = NY * PIECE
SMALL = PIECE // 8
TOP = [(z, (6, 7, 4, 5, 2, 3, 0, 1)[z]) for z in range(NZ)]
SIDE = [(z, (z - 1 if z % 2 == 0 else z + 1) % NZ) for z in range(NZ)]
Y_ORDER = (1, 2, 3)
POOL = 5 * 10**9
FIRST = 5 * 10**9
FINAL = 5*10**9
EARLY_STACK = True
ROOT_HALF = 0.7071067811865476
SCALE = 1.0 / math.sqrt(D)
SCALE_LOG2E = SCALE * math.log2(math.e)
BF = jnp.bfloat16
F32 = jnp.float32

AT1 = PLANE
AT2 = AT1 + PLANE // 2
AT3 = AT2 + PLANE // 4
COLS = AT3 + 2 * B
PAIR = 8 * B


def dot(a, b, ca=1, cb=0):
    return lax.dot_general(a, b, (((ca,), (cb,)), ((), ())), preferred_element_type=F32)


def pair_sum(rows):
    r = lax.broadcasted_iota(jnp.int32, (rows, 2 * rows), 0)
    c = lax.broadcasted_iota(jnp.int32, (rows, 2 * rows), 1)
    return (lax.shift_right_logical(c, 1) == r).astype(F32).astype(BF)


def repeat_matrix(rows, log):
    r = lax.broadcasted_iota(jnp.int32, (rows << log, rows), 0)
    c = lax.broadcasted_iota(jnp.int32, (rows << log, rows), 1)
    return (lax.shift_right_logical(r, log) == c).astype(F32).astype(BF)


def pool(matrix, x):
    return (dot(matrix, x) * ROOT_HALF).astype(BF)


def expand(matrix, x):
    high = x.astype(BF)
    low = (x - high.astype(F32)).astype(BF)
    return dot(matrix, high) + dot(matrix, low)


def part_at(index, size=PIECE):
    return pl.ds(pl.multiple_of(index * size, size), size)


def head_at(index):
    return pl.ds(pl.multiple_of(index * D, D), D)


def later(y, d):
    return lax.rem(y + d, NY)


def earlier(y, d):
    return lax.rem(y - d + NY, NY)


def first_kernel(token_ref):
    token_ref[...] = jnp.zeros_like(token_ref)


def pack_kernel(left_hbm, right_hbm, *refs):
    outs, sems = refs[:NY], refs[-1]
    y = lax.axis_index("y")
    copies = [
        pltpu.make_async_copy(
            src.at[:, head_at(later(y, d))], outs[d].at[:, n * D : (n + 1) * D], sems.at[d, n]
        )
        for d in range(NY)
        for n, src in enumerate((left_hbm, right_hbm))
    ]
    for copy in copies:
        copy.start()
    for copy in copies:
        copy.wait()


def stack_kernel(left_hbm, right_hbm, out_ref, sems):
    copies = [
        pltpu.make_async_copy(
            src.at[:, h * D : (h + 1) * D],
            out_ref.at[h * PIECE : (h + 1) * PIECE, n * D : (n + 1) * D],
            sems.at[h, n],
        )
        for h in range(NY)
        for n, src in enumerate((left_hbm, right_hbm))
    ]
    for copy in copies:
        copy.start()
    for copy in copies:
        copy.wait()


def unstack_kernel(in_ref, left_hbm, right_hbm, token_ref, sems):
    token_ref[...] = jnp.zeros_like(token_ref)
    copies = [
        pltpu.make_async_copy(
            in_ref.at[h * PIECE : (h + 1) * PIECE, n * D : (n + 1) * D],
            dst.at[:, h * D : (h + 1) * D],
            sems.at[h, n],
        )
        for h in range(NY)
        for n, dst in enumerate((left_hbm, right_hbm))
    ]
    for copy in copies:
        copy.start()
    for copy in copies:
        copy.wait()


def unpack_kernel(*refs):
    pieces, left_hbm, right_hbm, sems = refs[:NY], refs[NY], refs[NY + 1], refs[-1]
    y = lax.axis_index("y")
    copies = [
        pltpu.make_async_copy(
            pieces[d].at[:, n * D : (n + 1) * D], dst.at[:, head_at(earlier(y, d))], sems.at[d, n]
        )
        for d in range(NY)
        for n, dst in enumerate((left_hbm, right_hbm))
    ]
    for copy in copies:
        copy.start()
    for copy in copies:
        copy.wait()


def pool_kernel(k0, k1, k2, k3, kv_ref, m1_ref, four_ref, side_ref):
    y = lax.axis_index("y")
    odd = lax.rem(lax.axis_index("z"), 2)
    for d, ref in enumerate((k0, k1, k2, k3)):
        kv_ref[part_at(earlier(y, d)), :] = ref[...]
    matrix = pair_sum(B)
    one = [pool(matrix, kv_ref[n * PIECE : (n + 1) * PIECE]) for n in range(4)]
    two = [pool(matrix, jnp.concatenate(one[n : n + 2], axis=0)) for n in (0, 2)]
    three = pool(matrix, jnp.concatenate(two, axis=0))
    four = pool(matrix[:HALF, :B], three)
    facing = kv_ref[part_at((1 - odd) * (PLANE // B - 1), B), :]
    other = kv_ref[part_at(odd * (PLANE // B - 1), B), :]
    m1_ref[:B] = three
    m1_ref[B:] = facing
    four_ref[...] = four
    side_ref[...] = other


def quad_kernel(own_four, three_1, four_2, four_3, top_ref):
    z = lax.axis_index("z")
    matrix = pair_sum(HALF)
    small = matrix[: B // 4, :HALF]
    fours = (own_four[...], pool(matrix, three_1[:B]), four_2[...], four_3[...])
    for d, four in enumerate(fours):
        top_ref[part_at((z ^ d) & 3, SMALL), :] = pool(small, four)


def by_three(z):
    return lax.rem(lax.shift_right_logical(z + 1, 1), 2) == 1


def pieces_of(i):
    start = max(0, i * PIECE - B)
    stop = min(PLANE, i * PIECE + 3 * B)
    return (
        (start, stop - start, start - (i * PIECE - B)),
        (AT1 + (i ^ 1) * B, B, 4 * B),
        (AT2 + ((i >> 1) ^ 1) * B, B, 5 * B),
        (AT3, 2 * B, 6 * B),
    )


def summed(values):
    return functools.reduce(jnp.add, values)


def early_kernel(
    kv, from_1, from_2, from_3, qc, keys_t, vals_t, raised, pgrads, stats, keys, vals
):
    matrix = pair_sum(B)
    one = [pool(matrix, kv[n * PIECE : (n + 1) * PIECE]) for n in range(4)]
    two = [pool(matrix, jnp.concatenate(one[n : n + 2], axis=0)) for n in (0, 2)]
    at = 0
    for part in (kv[...], *one, *two, from_1[:B], from_2[...], from_3[...]):
        rows = part.shape[0]
        keys[at : at + rows, :] = part[:, :D]
        vals[at : at + rows, :] = part[:, D:]
        at += rows
    second = lax.broadcasted_iota(jnp.int32, (B, PIECE), 1) >= B
    for i in range(NY):
        lanes = slice(i * PIECE, (i + 1) * PIECE)
        q = qc[lanes, :D]
        c = qc[lanes, D:]
        pieces = pieces_of(i)
        scores = [dot(keys[a : a + n, :], q, 1, 1) for a, n, _ in pieces]
        near = [scores[0][m * B : (m + 1) * B] for m in range(pieces[0][1] // B)]
        if i > 0:
            near[0] = jnp.where(second, -jnp.inf, near[0])
        if i < NY - 1:
            near[-1] = jnp.where(second, near[-1], -jnp.inf)
        scores[0] = jnp.concatenate(near, axis=0)
        top = functools.reduce(jnp.maximum, [jnp.max(s, axis=0, keepdims=True) for s in scores])
        total = []
        weighted = []
        for (a, n, r), s in zip(pieces, scores):
            e = jnp.exp2((s - top) * SCALE_LOG2E)
            g = dot(vals[a : a + n, :], c, 1, 1)
            raised[i, r : r + n, :] = e
            pgrads[i, r : r + n, :] = g
            total.append(jnp.sum(e, axis=0, keepdims=True))
            weighted.append(jnp.sum(e * g, axis=0, keepdims=True))
        stats[0:1, lanes] = top
        stats[1:2, lanes] = summed(total)
        stats[2:3, lanes] = summed(weighted)
    for n in range(COLS // B):
        cut = slice(n * B, (n + 1) * B)
        keys_t[:, cut] = keys[cut, :].T
        vals_t[:, cut] = vals[cut, :].T


def late_kernel(
    from_1, from_side, from_7, qc, stats, top_ref, g_facing, g_other, edges, found, w5, s5, ew, es
):
    z = lax.axis_index("z")
    odd = lax.rem(z, 2)
    edges[1 - odd] = from_1[B:]
    edges[odd] = from_side[...]
    first = lax.broadcasted_iota(jnp.int32, (B, PIECE), 1) < B
    for i in range(NY):
        lanes = slice(i * PIECE, (i + 1) * PIECE)
        q = qc[lanes, :D]
        c = qc[lanes, D:]
        scores = [dot(from_7[:B, :D], q, 1, 1)]
        pgrads = [dot(from_7[:B, D:], c, 1, 1)]
        side = {0: 0, NY - 1: 1}.get(i)
        if side is not None:
            score = dot(edges[side, :, :D], q, 1, 1)
            seen = first & (z > 0) if side == 0 else jnp.logical_not(first) & (z < NZ - 1)
            scores.append(jnp.where(seen, score, -jnp.inf))
            pgrads.append(dot(edges[side, :, D:], c, 1, 1))
        before = stats[0:1, lanes]
        top = functools.reduce(
            jnp.maximum, [before] + [jnp.max(s, axis=0, keepdims=True) for s in scores]
        )
        raised = [jnp.exp2((s - top) * SCALE_LOG2E) for s in scores]
        shrink = jnp.exp2((before - top) * SCALE_LOG2E)
        total = shrink * stats[1:2, lanes] + summed(
            [jnp.sum(e, axis=0, keepdims=True) for e in raised]
        )
        weighted = shrink * stats[2:3, lanes] + summed(
            [jnp.sum(e * g, axis=0, keepdims=True) for e, g in zip(raised, pgrads)]
        )
        inverse = 1.0 / total
        row_dot = inverse * weighted
        found[0:1, lanes] = shrink * inverse
        found[1:2, lanes] = row_dot
        probs = [e * inverse for e in raised]
        sgrads = [(p * (g - row_dot) * SCALE).astype(BF) for p, g in zip(probs, pgrads)]
        w5[:, lanes] = probs[0].astype(BF)
        s5[:, lanes] = sgrads[0]
        if side is not None:
            ew[side] = probs[1].astype(BF)
            es[side] = sgrads[1]
    top_ref[:B, :D] = dot(s5[...], qc[:, :D]).astype(BF)
    top_ref[:B, D:] = dot(w5[...], qc[:, D:]).astype(BF)

    def edge_grads(side):
        lanes = part_at(side * (NY - 1))
        key = dot(es[side], qc[lanes, :D]).astype(BF)
        value = dot(ew[side], qc[lanes, D:]).astype(BF)
        return key, value

    g_facing[:, :D], g_facing[:, D:] = edge_grads(1 - odd)
    key, value = edge_grads(odd)
    top_ref[B:, :D] = key
    top_ref[B:, D:] = value
    g_other[:, :D] = key
    g_other[:, D:] = value


def rest_kernel(
    keys_t, vals_t, raised, pgrads, qc, from_7, edges, found, w5, s5, ew, es,
    og, g4, g3, g_own, g_one, g_two, grads,
):
    grads[...] = jnp.zeros_like(grads)
    five_k = from_7[:B, :D].T
    five_v = from_7[:B, D:].T
    for i in range(NY):
        lanes = slice(i * PIECE, (i + 1) * PIECE)
        q = qc[lanes, :D]
        c = qc[lanes, D:]
        ratio = found[0:1, lanes]
        row_dot = found[1:2, lanes]
        out_t = [dot(five_v, w5[:, lanes])]
        qg_t = [dot(five_k, s5[:, lanes])]
        side = {0: 0, NY - 1: 1}.get(i)
        if side is not None:
            out_t.append(dot(edges[side, :, D:].T, ew[side]))
            qg_t.append(dot(edges[side, :, :D].T, es[side]))
        for a, n, r in pieces_of(i):
            p = raised[i, r : r + n, :] * ratio
            w = p.astype(BF)
            s = (p * (pgrads[i, r : r + n, :] - row_dot) * SCALE).astype(BF)
            out_t.append(dot(vals_t[:, a : a + n], w))
            qg_t.append(dot(keys_t[:, a : a + n], s))
            grads[a : a + n, :D] += dot(s, q)
            grads[a : a + n, D:] += dot(w, c)
        og[lanes, :D] = summed(out_t).T.astype(BF)
        og[lanes, D:] = summed(qg_t).T.astype(BF)
    g_own[...] = grads[:AT1]
    g_one[...] = grads[AT1:AT2]
    g_two[...] = grads[AT2:AT3]
    g3[...] = grads[AT3 : AT3 + B]
    g4[...] = grads[AT3 + B :]


def spread_kernel(
    back_ref, g4_ref, g3_ref, facing_ref, other_ref, s1_ref, s2_ref, s3_ref, keep_ref
):
    z = lax.axis_index("z")
    twice = repeat_matrix(B // 4, 1)
    fourfold = repeat_matrix(B // 4, 2)

    def rows(d):
        return back_ref[part_at((z ^ d) & 3, SMALL), :]

    s1_ref[:B] = (g3_ref[...] + dot(fourfold, rows(1)) * 0.5).astype(BF)
    s1_ref[B:] = facing_ref[...]
    s2_ref[...] = (g4_ref[:HALF] + dot(twice, rows(2)) * ROOT_HALF).astype(BF)
    s3_ref[:HALF] = (g4_ref[HALF:] + dot(twice, rows(3)) * ROOT_HALF).astype(BF)
    s3_ref[HALF:] = other_ref[...]
    keep_ref[...] = dot(fourfold, rows(0)) * 0.5


def local_kernel(own_ref, one_ref, two_ref, out_ref, *_):
    matrix = repeat_matrix(B, 1)
    for n in range(2):
        two = expand(matrix, two_ref[n * B : (n + 1) * B] * ROOT_HALF)
        for m in range(2):
            k = 2 * n + m
            one = one_ref[k * B : (k + 1) * B] + two[m * B : (m + 1) * B]
            cut = slice(k * PIECE, (k + 1) * PIECE)
            out_ref[cut] = own_ref[cut] + expand(matrix, one * ROOT_HALF)


def final_kernel(own_ref, keep_ref, b1_ref, b2_ref, b3_ref, b7_ref, f0, f1, f2, f3, total):
    y = lax.axis_index("y")
    z = lax.axis_index("z")
    odd = lax.rem(z, 2)
    four = (b2_ref[...].astype(F32) + b3_ref[:HALF].astype(F32)) * ROOT_HALF
    up = keep_ref[...] + b1_ref[:B].astype(F32) + expand(repeat_matrix(HALF, 1), four)
    up *= ROOT_HALF * 0.5
    matrix = repeat_matrix(SMALL, 3)
    for n in range(NY):
        cut = slice(n * PIECE, (n + 1) * PIECE)
        total[cut] = own_ref[cut] + expand(matrix, up[n * SMALL : (n + 1) * SMALL])
    facing = part_at((1 - odd) * (PLANE // B - 1), B)
    total[facing, :] += b1_ref[B:].astype(F32)
    other = part_at(odd * (PLANE // B - 1), B)
    total[other, :] += jnp.where(by_three(z), b3_ref[HALF:], b7_ref[B:]).astype(F32)
    for d, ref in enumerate((f0, f1, f2, f3)):
        ref[...] = total[part_at(later(y, d)), :].astype(BF)


VMEM = pl.BlockSpec(memory_space=pltpu.VMEM)
ANY = pl.BlockSpec(memory_space=pl.ANY)
HBM = pl.BlockSpec(memory_space=pltpu.HBM)


TOKEN = ((8, 128), F32)


def call(kernel, ins, outs, scratch=(), flops=10**6, source=VMEM, target=VMEM, after=(), vmem=8, alias=None):
    size = sum(a.size * a.dtype.itemsize for a in ins)
    size += sum(math.prod(s) * jnp.dtype(t).itemsize for s, t in outs)
    count = len(ins)

    def body(*refs):
        kernel(*refs[:count], *refs[count + len(after) :])

    return pl.pallas_call(
        body,
        out_shape=[jax.ShapeDtypeStruct(s, t) for s, t in outs],
        in_specs=[source] * count + [ANY] * len(after),
        out_specs=[target if s != TOKEN else VMEM for s in outs[: len(outs) - bool(alias)]]
        + [ANY] * bool(alias),
        scratch_shapes=list(scratch),
        input_output_aliases=alias or {},
        compiler_params=pltpu.CompilerParams(vmem_limit_bytes=vmem * 2**20),
        cost_estimate=pl.CostEstimate(flops=flops, bytes_accessed=size, transcendentals=0),
    )(*ins, *after)


def around_y(pieces):
    got = {0: pieces[0]}
    for d in Y_ORDER:
        got[d] = lax.ppermute(pieces[d], "y", [(i, (i + d) % NY) for i in range(NY)])
    return [got[d] for d in range(NY)]


def across_y(array):
    return lax.all_to_all(array, "y", split_axis=0, concat_axis=0, tiled=True)


def over_z(array, d):
    return lax.ppermute(array, "z", [(i, i ^ d) for i in range(NZ)])


def per_device(queries, keys, values, cotangent):
    piece = ((PIECE, 2 * D), BF)
    plane = ((PLANE, 2 * D), BF)
    level = ((B, 2 * D), BF)
    half = ((HALF, 2 * D), BF)
    tail = ((HALF + B, 2 * D), BF)
    double = ((2 * B, 2 * D), BF)
    wide = ((B, 2 * D), F32)
    sems = [pltpu.SemaphoreType.DMA((NY, 2))]
    (token,) = call(first_kernel, [], [TOKEN], flops=FIRST)
    kv = call(
        pack_kernel, [keys, values], [piece] * NY, scratch=sems, source=HBM, flops=5 * 10**9, after=[token]
    )
    kv = around_y(kv)
    (qc_own,) = call(stack_kernel, [queries, cotangent], [plane], scratch=sems, source=HBM)
    qc = across_y(qc_own)
    kv, m1, four, side = call(
        pool_kernel,
        [*kv],
        [plane, double, half, level],
        flops=POOL,
        after=[qc_own],
    )
    from_1, from_2, from_3 = over_z(m1, 1), over_z(four, 2), over_z(four, 3)
    from_side = lax.ppermute(side, "z", SIDE)
    (top,) = call(quad_kernel, [four, from_1, from_2, from_3], [level])
    from_7 = lax.ppermute(top, "z", TOP)
    keys_t, vals_t, raised, pgrads, stats = call(
        early_kernel,
        [kv, from_1, from_2, from_3, qc],
        [((D, COLS), BF)] * 2 + [((NY, PAIR, PIECE), F32)] * 2 + [((8, PLANE), F32)],
        scratch=[pltpu.VMEM((COLS, D), BF)] * 2,
        flops=10**9,
        vmem=20,
    )
    g_top, g_facing, g_other, edges, found, w5, s5, ew, es = call(
        late_kernel,
        [from_1, from_side, from_7, qc, stats],
        [double, level, level, ((2, B, 2 * D), BF), ((8, PLANE), F32)]
        + [((B, PLANE), BF)] * 2
        + [((2, B, PIECE), BF)] * 2,
        flops=10**8,
    )
    og, g4, g3, g_own, g_one, g_two = call(
        rest_kernel,
        [keys_t, vals_t, raised, pgrads, qc, from_7, edges, found, w5, s5, ew, es],
        [plane, wide, wide]
        + [((PLANE, 2 * D), F32), ((PLANE // 2, 2 * D), F32), ((PLANE // 4, 2 * D), F32)],
        scratch=[pltpu.VMEM((COLS, 2 * D), F32)],
        flops=2 * 10**9,
        vmem=20,
    )
    back_7 = over_z(g_top, 7)
    s1, s2, s3, keep = call(
        spread_kernel,
        [back_7, g4, g3, g_facing, g_other],
        [double, half, tail, wide],
    )
    own, og = call(
        local_kernel,
        [g_own, g_one, g_two],
        [((PLANE, 2 * D), F32), plane],
        after=[og, keep],
        alias={3: 1},
    )
    og = across_y(og)
    back_1, back_2, back_3 = over_z(s1, 1), over_z(s2, 2), over_z(s3, 3)
    whole = ((PIECE, NY * D), BF)
    attended, grad_queries, token = call(
        unstack_kernel, [og], [whole] * 2 + [TOKEN], scratch=sems, target=HBM
    )
    final = call(
        final_kernel,
        [own, keep, back_1, back_2, back_3, back_7],
        [piece] * NY,
        scratch=[pltpu.VMEM((PLANE, 2 * D), F32)],
        flops=FINAL,
    )
    final = around_y(final)
    grad_keys, grad_values = call(
        unpack_kernel, [*final], [whole] * 2, scratch=sems, target=HBM, after=[token]
    )
    return attended, grad_queries, grad_keys, grad_values


def solution(mesh):
    seq, head, rep = mesh.devices.shape
    split = Mesh(mesh.devices.reshape(NZ, NY, head, rep), ("z", "y", "head", "rep"))
    spec = P(("rep", "z", "y"), "head")
    return jax.shard_map(
        per_device, mesh=split, in_specs=(spec,) * 4, out_specs=(spec,) * 4, check_vma=False
    )
```

```python
import functools
import math

import jax
import jax.numpy as jnp
from jax import lax
from jax.experimental import pallas as pl
from jax.experimental.pallas import tpu as pltpu
from jax.sharding import Mesh
from jax.sharding import PartitionSpec as P

D = 128
B = 128
HALF = B // 2
NY = 4
NZ = 8
PIECE = 2 * B
PLANE = NY * PIECE
SMALL = PIECE // 8
TOP = [(z, (6, 7, 4, 5, 2, 3, 0, 1)[z]) for z in range(NZ)]
SIDE = [(z, (z - 1 if z % 2 == 0 else z + 1) % NZ) for z in range(NZ)]
Y_ORDER = (1, 2, 3)
POOL = 5 * 10**9
FIRST = 5 * 10**9
FINAL = 5*10**9
EARLY_STACK = True
ROOT_HALF = 0.7071067811865476
SCALE = 1.0 / math.sqrt(D)
SCALE_LOG2E = SCALE * math.log2(math.e)
BF = jnp.bfloat16
F32 = jnp.float32

AT1 = PLANE
AT2 = AT1 + PLANE // 2
AT3 = AT2 + PLANE // 4
COLS = AT3 + 2 * B
PAIR = 8 * B


def dot(a, b, ca=1, cb=0):
    return lax.dot_general(a, b, (((ca,), (cb,)), ((), ())), preferred_element_type=F32)


def pair_sum(rows):
    r = lax.broadcasted_iota(jnp.int32, (rows, 2 * rows), 0)
    c = lax.broadcasted_iota(jnp.int32, (rows, 2 * rows), 1)
    return (lax.shift_right_logical(c, 1) == r).astype(F32).astype(BF)


def repeat_matrix(rows, log):
    r = lax.broadcasted_iota(jnp.int32, (rows << log, rows), 0)
    c = lax.broadcasted_iota(jnp.int32, (rows << log, rows), 1)
    return (lax.shift_right_logical(r, log) == c).astype(F32).astype(BF)


def pool(matrix, x):
    return (dot(matrix, x) * ROOT_HALF).astype(BF)


def expand(matrix, x):
    high = x.astype(BF)
    low = (x - high.astype(F32)).astype(BF)
    return dot(matrix, high) + dot(matrix, low)


def part_at(index, size=PIECE):
    return pl.ds(pl.multiple_of(index * size, size), size)


def head_at(index):
    return pl.ds(pl.multiple_of(index * D, D), D)


def later(y, d):
    return lax.rem(y + d, NY)


def earlier(y, d):
    return lax.rem(y - d + NY, NY)


def first_kernel(token_ref):
    token_ref[...] = jnp.zeros_like(token_ref)


def pack_kernel(left_hbm, right_hbm, *refs):
    outs, sems = refs[:NY], refs[-1]
    y = lax.axis_index("y")
    copies = [
        pltpu.make_async_copy(
            src.at[:, head_at(later(y, d))], outs[d].at[:, n * D : (n + 1) * D], sems.at[d, n]
        )
        for d in range(NY)
        for n, src in enumerate((left_hbm, right_hbm))
    ]
    for copy in copies:
        copy.start()
    for copy in copies:
        copy.wait()


def stack_kernel(left_hbm, right_hbm, out_ref, sems):
    copies = [
        pltpu.make_async_copy(
            src.at[:, h * D : (h + 1) * D],
            out_ref.at[h * PIECE : (h + 1) * PIECE, n * D : (n + 1) * D],
            sems.at[h, n],
        )
        for h in range(NY)
        for n, src in enumerate((left_hbm, right_hbm))
    ]
    for copy in copies:
        copy.start()
    for copy in copies:
        copy.wait()


def unstack_kernel(in_ref, left_hbm, right_hbm, token_ref, sems):
    token_ref[...] = jnp.zeros_like(token_ref)
    copies = [
        pltpu.make_async_copy(
            in_ref.at[h * PIECE : (h + 1) * PIECE, n * D : (n + 1) * D],
            dst.at[:, h * D : (h + 1) * D],
            sems.at[h, n],
        )
        for h in range(NY)
        for n, dst in enumerate((left_hbm, right_hbm))
    ]
    for copy in copies:
        copy.start()
    for copy in copies:
        copy.wait()


def unpack_kernel(*refs):
    pieces, left_hbm, right_hbm, sems = refs[:NY], refs[NY], refs[NY + 1], refs[-1]
    y = lax.axis_index("y")
    copies = [
        pltpu.make_async_copy(
            pieces[d].at[:, n * D : (n + 1) * D], dst.at[:, head_at(earlier(y, d))], sems.at[d, n]
        )
        for d in range(NY)
        for n, dst in enumerate((left_hbm, right_hbm))
    ]
    for copy in copies:
        copy.start()
    for copy in copies:
        copy.wait()


def pool_kernel(k0, k1, k2, k3, kv_ref, m1_ref, four_ref, side_ref):
    y = lax.axis_index("y")
    odd = lax.rem(lax.axis_index("z"), 2)
    for d, ref in enumerate((k0, k1, k2, k3)):
        kv_ref[part_at(earlier(y, d)), :] = ref[...]
    matrix = pair_sum(B)
    one = [pool(matrix, kv_ref[n * PIECE : (n + 1) * PIECE]) for n in range(4)]
    two = [pool(matrix, jnp.concatenate(one[n : n + 2], axis=0)) for n in (0, 2)]
    three = pool(matrix, jnp.concatenate(two, axis=0))
    four = pool(matrix[:HALF, :B], three)
    facing = kv_ref[part_at((1 - odd) * (PLANE // B - 1), B), :]
    other = kv_ref[part_at(odd * (PLANE // B - 1), B), :]
    m1_ref[:B] = three
    m1_ref[B:] = facing
    four_ref[...] = four
    side_ref[...] = other


def quad_kernel(own_four, three_1, four_2, four_3, top_ref):
    z = lax.axis_index("z")
    matrix = pair_sum(HALF)
    small = matrix[: B // 4, :HALF]
    fours = (own_four[...], pool(matrix, three_1[:B]), four_2[...], four_3[...])
    for d, four in enumerate(fours):
        top_ref[part_at((z ^ d) & 3, SMALL), :] = pool(small, four)


def by_three(z):
    return lax.rem(lax.shift_right_logical(z + 1, 1), 2) == 1


def pieces_of(i):
    start = max(0, i * PIECE - B)
    stop = min(PLANE, i * PIECE + 3 * B)
    return (
        (start, stop - start, start - (i * PIECE - B)),
        (AT1 + (i ^ 1) * B, B, 4 * B),
        (AT2 + ((i >> 1) ^ 1) * B, B, 5 * B),
        (AT3, 2 * B, 6 * B),
    )


def summed(values):
    return functools.reduce(jnp.add, values)


def early_kernel(
    kv, from_1, from_2, from_3, qc, keys_t, vals_t, raised, pgrads, stats, keys, vals
):
    matrix = pair_sum(B)
    one = [pool(matrix, kv[n * PIECE : (n + 1) * PIECE]) for n in range(4)]
    two = [pool(matrix, jnp.concatenate(one[n : n + 2], axis=0)) for n in (0, 2)]
    at = 0
    for part in (kv[...], *one, *two, from_1[:B], from_2[...], from_3[...]):
        rows = part.shape[0]
        keys[at : at + rows, :] = part[:, :D]
        vals[at : at + rows, :] = part[:, D:]
        at += rows
    second = lax.broadcasted_iota(jnp.int32, (B, PIECE), 1) >= B
    for i in range(NY):
        lanes = slice(i * PIECE, (i + 1) * PIECE)
        q = qc[lanes, :D]
        c = qc[lanes, D:]
        pieces = pieces_of(i)
        scores = [dot(keys[a : a + n, :], q, 1, 1) for a, n, _ in pieces]
        near = [scores[0][m * B : (m + 1) * B] for m in range(pieces[0][1] // B)]
        if i > 0:
            near[0] = jnp.where(second, -jnp.inf, near[0])
        if i < NY - 1:
            near[-1] = jnp.where(second, near[-1], -jnp.inf)
        scores[0] = jnp.concatenate(near, axis=0)
        top = functools.reduce(jnp.maximum, [jnp.max(s, axis=0, keepdims=True) for s in scores])
        total = []
        weighted = []
        for (a, n, r), s in zip(pieces, scores):
            e = jnp.exp2((s - top) * SCALE_LOG2E)
            g = dot(vals[a : a + n, :], c, 1, 1)
            raised[i, r : r + n, :] = e
            pgrads[i, r : r + n, :] = g
            total.append(jnp.sum(e, axis=0, keepdims=True))
            weighted.append(jnp.sum(e * g, axis=0, keepdims=True))
        stats[0:1, lanes] = top
        stats[1:2, lanes] = summed(total)
        stats[2:3, lanes] = summed(weighted)
    for n in range(COLS // B):
        cut = slice(n * B, (n + 1) * B)
        keys_t[:, cut] = keys[cut, :].T
        vals_t[:, cut] = vals[cut, :].T


def late_kernel(
    from_1, from_side, from_7, qc, stats, top_ref, g_facing, g_other, edges, found, w5, s5, ew, es
):
    z = lax.axis_index("z")
    odd = lax.rem(z, 2)
    edges[1 - odd] = from_1[B:]
    edges[odd] = from_side[...]
    first = lax.broadcasted_iota(jnp.int32, (B, PIECE), 1) < B
    for i in range(NY):
        lanes = slice(i * PIECE, (i + 1) * PIECE)
        q = qc[lanes, :D]
        c = qc[lanes, D:]
        scores = [dot(from_7[:B, :D], q, 1, 1)]
        pgrads = [dot(from_7[:B, D:], c, 1, 1)]
        side = {0: 0, NY - 1: 1}.get(i)
        if side is not None:
            score = dot(edges[side, :, :D], q, 1, 1)
            seen = first & (z > 0) if side == 0 else jnp.logical_not(first) & (z < NZ - 1)
            scores.append(jnp.where(seen, score, -jnp.inf))
            pgrads.append(dot(edges[side, :, D:], c, 1, 1))
        before = stats[0:1, lanes]
        top = functools.reduce(
            jnp.maximum, [before] + [jnp.max(s, axis=0, keepdims=True) for s in scores]
        )
        raised = [jnp.exp2((s - top) * SCALE_LOG2E) for s in scores]
        shrink = jnp.exp2((before - top) * SCALE_LOG2E)
        total = shrink * stats[1:2, lanes] + summed(
            [jnp.sum(e, axis=0, keepdims=True) for e in raised]
        )
        weighted = shrink * stats[2:3, lanes] + summed(
            [jnp.sum(e * g, axis=0, keepdims=True) for e, g in zip(raised, pgrads)]
        )
        inverse = 1.0 / total
        row_dot = inverse * weighted
        found[0:1, lanes] = shrink * inverse
        found[1:2, lanes] = row_dot
        probs = [e * inverse for e in raised]
        sgrads = [(p * (g - row_dot) * SCALE).astype(BF) for p, g in zip(probs, pgrads)]
        w5[:, lanes] = probs[0].astype(BF)
        s5[:, lanes] = sgrads[0]
        if side is not None:
            ew[side] = probs[1].astype(BF)
            es[side] = sgrads[1]
    top_ref[:B, :D] = dot(s5[...], qc[:, :D]).astype(BF)
    top_ref[:B, D:] = dot(w5[...], qc[:, D:]).astype(BF)

    def edge_grads(side):
        lanes = part_at(side * (NY - 1))
        key = dot(es[side], qc[lanes, :D]).astype(BF)
        value = dot(ew[side], qc[lanes, D:]).astype(BF)
        return key, value

    g_facing[:, :D], g_facing[:, D:] = edge_grads(1 - odd)
    key, value = edge_grads(odd)
    top_ref[B:, :D] = key
    top_ref[B:, D:] = value
    g_other[:, :D] = key
    g_other[:, D:] = value


def rest_kernel(
    keys_t, vals_t, raised, pgrads, qc, from_7, edges, found, w5, s5, ew, es,
    og, g4, g3, g_own, g_one, g_two, grads,
):
    grads[...] = jnp.zeros_like(grads)
    five_k = from_7[:B, :D].T
    five_v = from_7[:B, D:].T
    for i in range(NY):
        lanes = slice(i * PIECE, (i + 1) * PIECE)
        q = qc[lanes, :D]
        c = qc[lanes, D:]
        ratio = found[0:1, lanes]
        row_dot = found[1:2, lanes]
        out_t = [dot(five_v, w5[:, lanes])]
        qg_t = [dot(five_k, s5[:, lanes])]
        side = {0: 0, NY - 1: 1}.get(i)
        if side is not None:
            out_t.append(dot(edges[side, :, D:].T, ew[side]))
            qg_t.append(dot(edges[side, :, :D].T, es[side]))
        for a, n, r in pieces_of(i):
            p = raised[i, r : r + n, :] * ratio
            w = p.astype(BF)
            s = (p * (pgrads[i, r : r + n, :] - row_dot) * SCALE).astype(BF)
            out_t.append(dot(vals_t[:, a : a + n], w))
            qg_t.append(dot(keys_t[:, a : a + n], s))
            grads[a : a + n, :D] += dot(s, q)
            grads[a : a + n, D:] += dot(w, c)
        og[lanes, :D] = summed(out_t).T.astype(BF)
        og[lanes, D:] = summed(qg_t).T.astype(BF)
    g_own[...] = grads[:AT1]
    g_one[...] = grads[AT1:AT2]
    g_two[...] = grads[AT2:AT3]
    g3[...] = grads[AT3 : AT3 + B]
    g4[...] = grads[AT3 + B :]


def spread_kernel(
    back_ref, g4_ref, g3_ref, facing_ref, other_ref, s1_ref, s2_ref, s3_ref, keep_ref, *_
):
    z = lax.axis_index("z")
    twice = repeat_matrix(B // 4, 1)
    fourfold = repeat_matrix(B // 4, 2)

    def rows(d):
        return back_ref[part_at((z ^ d) & 3, SMALL), :]

    s1_ref[:B] = (g3_ref[...] + dot(fourfold, rows(1)) * 0.5).astype(BF)
    s1_ref[B:] = facing_ref[...]
    s2_ref[...] = (g4_ref[:HALF] + dot(twice, rows(2)) * ROOT_HALF).astype(BF)
    s3_ref[:HALF] = (g4_ref[HALF:] + dot(twice, rows(3)) * ROOT_HALF).astype(BF)
    s3_ref[HALF:] = other_ref[...]
    keep_ref[...] = dot(fourfold, rows(0)) * 0.5


def local_kernel(own_ref, one_ref, two_ref, out_ref):
    matrix = repeat_matrix(B, 1)
    for n in range(2):
        two = expand(matrix, two_ref[n * B : (n + 1) * B] * ROOT_HALF)
        for m in range(2):
            k = 2 * n + m
            one = one_ref[k * B : (k + 1) * B] + two[m * B : (m + 1) * B]
            cut = slice(k * PIECE, (k + 1) * PIECE)
            out_ref[cut] = own_ref[cut] + expand(matrix, one * ROOT_HALF)


def final_kernel(own_ref, keep_ref, b1_ref, b2_ref, b3_ref, b7_ref, f0, f1, f2, f3, total):
    y = lax.axis_index("y")
    z = lax.axis_index("z")
    odd = lax.rem(z, 2)
    four = (b2_ref[...].astype(F32) + b3_ref[:HALF].astype(F32)) * ROOT_HALF
    up = keep_ref[...] + b1_ref[:B].astype(F32) + expand(repeat_matrix(HALF, 1), four)
    up *= ROOT_HALF * 0.5
    matrix = repeat_matrix(SMALL, 3)
    for n in range(NY):
        cut = slice(n * PIECE, (n + 1) * PIECE)
        total[cut] = own_ref[cut] + expand(matrix, up[n * SMALL : (n + 1) * SMALL])
    facing = part_at((1 - odd) * (PLANE // B - 1), B)
    total[facing, :] += b1_ref[B:].astype(F32)
    other = part_at(odd * (PLANE // B - 1), B)
    total[other, :] += jnp.where(by_three(z), b3_ref[HALF:], b7_ref[B:]).astype(F32)
    for d, ref in enumerate((f0, f1, f2, f3)):
        ref[...] = total[part_at(later(y, d)), :].astype(BF)


VMEM = pl.BlockSpec(memory_space=pltpu.VMEM)
ANY = pl.BlockSpec(memory_space=pl.ANY)
HBM = pl.BlockSpec(memory_space=pltpu.HBM)


TOKEN = ((8, 128), F32)


def call(kernel, ins, outs, scratch=(), flops=10**6, source=VMEM, target=VMEM, after=(), vmem=8, alias=None):
    size = sum(a.size * a.dtype.itemsize for a in ins)
    size += sum(math.prod(s) * jnp.dtype(t).itemsize for s, t in outs)
    count = len(ins)

    def body(*refs):
        kernel(*refs[:count], *refs[count + len(after) :])

    return pl.pallas_call(
        body,
        out_shape=[jax.ShapeDtypeStruct(s, t) for s, t in outs],
        in_specs=[source] * count + [ANY] * len(after),
        out_specs=[target if s != TOKEN else VMEM for s in outs[: len(outs) - bool(alias)]]
        + [ANY] * bool(alias),
        scratch_shapes=list(scratch),
        input_output_aliases=alias or {},
        compiler_params=pltpu.CompilerParams(vmem_limit_bytes=vmem * 2**20),
        cost_estimate=pl.CostEstimate(flops=flops, bytes_accessed=size, transcendentals=0),
    )(*ins, *after)


def around_y(pieces):
    got = {0: pieces[0]}
    for d in Y_ORDER:
        got[d] = lax.ppermute(pieces[d], "y", [(i, (i + d) % NY) for i in range(NY)])
    return [got[d] for d in range(NY)]


def across_y(array):
    return lax.all_to_all(array, "y", split_axis=0, concat_axis=0, tiled=True)


def over_z(array, d):
    return lax.ppermute(array, "z", [(i, i ^ d) for i in range(NZ)])


def per_device(queries, keys, values, cotangent):
    piece = ((PIECE, 2 * D), BF)
    plane = ((PLANE, 2 * D), BF)
    level = ((B, 2 * D), BF)
    half = ((HALF, 2 * D), BF)
    tail = ((HALF + B, 2 * D), BF)
    double = ((2 * B, 2 * D), BF)
    wide = ((B, 2 * D), F32)
    sems = [pltpu.SemaphoreType.DMA((NY, 2))]
    (token,) = call(first_kernel, [], [TOKEN], flops=FIRST)
    kv = call(
        pack_kernel, [keys, values], [piece] * NY, scratch=sems, source=HBM, flops=5 * 10**9, after=[token]
    )
    kv = around_y(kv)
    (qc_own,) = call(stack_kernel, [queries, cotangent], [plane], scratch=sems, source=HBM)
    qc = across_y(qc_own)
    kv, m1, four, side = call(
        pool_kernel,
        [*kv],
        [plane, double, half, level],
        flops=POOL,
        after=[qc_own],
    )
    from_1, from_2, from_3 = over_z(m1, 1), over_z(four, 2), over_z(four, 3)
    from_side = lax.ppermute(side, "z", SIDE)
    (top,) = call(quad_kernel, [four, from_1, from_2, from_3], [level])
    from_7 = lax.ppermute(top, "z", TOP)
    keys_t, vals_t, raised, pgrads, stats = call(
        early_kernel,
        [kv, from_1, from_2, from_3, qc],
        [((D, COLS), BF)] * 2 + [((NY, PAIR, PIECE), F32)] * 2 + [((8, PLANE), F32)],
        scratch=[pltpu.VMEM((COLS, D), BF)] * 2,
        flops=10**9,
        vmem=20,
    )
    g_top, g_facing, g_other, edges, found, w5, s5, ew, es = call(
        late_kernel,
        [from_1, from_side, from_7, qc, stats],
        [double, level, level, ((2, B, 2 * D), BF), ((8, PLANE), F32)]
        + [((B, PLANE), BF)] * 2
        + [((2, B, PIECE), BF)] * 2,
        flops=10**8,
    )
    og, g4, g3, g_own, g_one, g_two = call(
        rest_kernel,
        [keys_t, vals_t, raised, pgrads, qc, from_7, edges, found, w5, s5, ew, es],
        [plane, wide, wide]
        + [((PLANE, 2 * D), F32), ((PLANE // 2, 2 * D), F32), ((PLANE // 4, 2 * D), F32)],
        scratch=[pltpu.VMEM((COLS, 2 * D), F32)],
        flops=2 * 10**9,
        vmem=20,
    )
    back_7 = over_z(g_top, 7)
    (own,) = call(local_kernel, [g_own, g_one, g_two], [((PLANE, 2 * D), F32)])
    s1, s2, s3, keep, og = call(
        spread_kernel,
        [back_7, g4, g3, g_facing, g_other],
        [double, half, tail, wide, plane],
        after=[og, own],
        alias={5: 4},
    )
    back_1, back_2, back_3 = over_z(s1, 1), over_z(s2, 2), over_z(s3, 3)
    og = across_y(og)
    back_1, back_2, back_3 = over_z(s1, 1), over_z(s2, 2), over_z(s3, 3)
    whole = ((PIECE, NY * D), BF)
    attended, grad_queries, token = call(
        unstack_kernel, [og], [whole] * 2 + [TOKEN], scratch=sems, target=HBM
    )
    final = call(
        final_kernel,
        [own, keep, back_1, back_2, back_3, back_7],
        [piece] * NY,
        scratch=[pltpu.VMEM((PLANE, 2 * D), F32)],
        flops=FINAL,
    )
    final = around_y(final)
    grad_keys, grad_values = call(
        unpack_kernel, [*final], [whole] * 2, scratch=sems, target=HBM, after=[token]
    )
    return attended, grad_queries, grad_keys, grad_values


def solution(mesh):
    seq, head, rep = mesh.devices.shape
    split = Mesh(mesh.devices.reshape(NZ, NY, head, rep), ("z", "y", "head", "rep"))
    spec = P(("rep", "z", "y"), "head")
    return jax.shard_map(
        per_device, mesh=split, in_specs=(spec,) * 4, out_specs=(spec,) * 4, check_vma=False
    )
```
